256 devices in a mesh: ha: 8 (over z), wa: 32 (over x, y, core).
Axes of the slice: x: 4, y: 4, z: 8, core: 2. Of those that a mesh axis runs over, the one named last changes fastest.
Arguments:
- tokens: bfloat16 [64, 512, 512], P('ha', 'wa'), may hold values from -6 to 6
- cotangent: bfloat16 [64, 512, 512], P('ha', 'wa'), may hold values from -6 to 6
- state_in: float32 [64, 512, 16], P('ha', 'wa'), may hold values from -0.25 to 0.25
- state_out: float32 [64, 512, 16], P('ha', 'wa'), may hold values from -0.25 to 0.25
- width_decay: float32 [64, 512, 8], P('ha', 'wa'), may hold values from -1.6 to 0
- height_decay: float32 [64, 512, 8], P('ha', 'wa'), may hold values from -1.6 to 0
Outputs:
- tokens_grad: float32 [64, 512, 512], P('ha', 'wa')
- state_in_grad: float32 [64, 512, 16], P('ha', 'wa')
- state_out_grad: float32 [64, 512, 16], P('ha', 'wa')
- width_decay_grad: float32 [64, 512, 8], P('ha', 'wa')
- height_decay_grad: float32 [64, 512, 8], P('ha', 'wa')
The draws below stay inside these ranges and needn't reach their ends.
All inputs are finite; a program needn't handle non-finite values.
Results may differ from the reference program's by a relative error of at most 0.0003.
Values sent between devices are 32-bit elements; how exact they have to be, the bound alone decides.
No kernel may reach another device: no remote copies, remote signals or barrier semaphores. Data moves between devices by JAX's collectives and lax.ppermute only.
A program may use at most 128 MiB of HBM per device.

```python
import jax
import jax.numpy as jnp
from jax import lax

D = 512
G = 8
N = 16
HEIGHT = 64
WIDTH = 512


def decay_logs(key, direction, sequence_length):
    key_list = jax.random.split(key, 7)
    fast_count = jax.random.randint(key_list[0], (), 2, 5)
    ranking = jax.random.permutation(key_list[1], G)
    is_fast = ranking < fast_count
    slow_rate = jax.random.uniform(key_list[2], (G,), jnp.float32, 0.1, 0.5) / sequence_length
    fast_rate = jnp.exp(jax.random.uniform(key_list[3], (G,), jnp.float32, jnp.log(1.0 / 50.0), jnp.log(1.0 / 30.0)))
    cluster_decay_rate = jnp.where(is_fast, fast_rate, slow_rate)
    texture_jitter = jnp.exp(jax.random.uniform(key_list[4], (HEIGHT, WIDTH, G), jnp.float32, jnp.log(0.5), jnp.log(2.0)))
    position_indices = jax.random.randint(key_list[5], (3,), 0, sequence_length)
    loss_values = jax.random.uniform(key_list[6], (3,), jnp.float32, 0.22, 0.51)
    spike_stripe_row = jnp.sum(loss_values[:, None] * (jnp.arange(sequence_length)[None, :] == position_indices[:, None]).astype(jnp.float32), axis=0)
    if direction == 1:
        spike_lattice = spike_stripe_row[None, :, None]
    else:
        spike_lattice = spike_stripe_row[:, None, None]
    return (-(cluster_decay_rate * texture_jitter + spike_lattice)).astype(jnp.float32)


def draw_width_decay(key, part):
    return decay_logs(jax.random.fold_in(key, 11), 1, WIDTH)


def draw_height_decay(key, part):
    return decay_logs(jax.random.fold_in(key, 23), 0, HEIGHT)


def steps_of(rng, shape, cuts, least, high):
    loudness = 1.0
    for axis_at, blocks in cuts:
        draws = jax.random.uniform(jax.random.fold_in(jax.random.fold_in(rng, 6), axis_at), (blocks,), jnp.float32, least / len(cuts), high / len(cuts))
        loudness = loudness * jnp.repeat(jnp.exp(draws), shape[axis_at] // blocks).reshape((-1,) + (1,) * (len(shape) - 1 - axis_at))
    return loudness


def centred(own_key, extent, scale, bound, cuts=(), kind=jnp.bfloat16):
    level = steps_of(own_key, extent, cuts, -0.22, 0.18) if cuts else 1.0
    entries = jax.random.normal(own_key, extent, jnp.float32) * scale * level
    return jnp.minimum(jnp.maximum(entries, -bound), bound).astype(kind)


def setup_inputs(seed: int = 0) -> dict:
    key_of = jax.random.split(jax.random.key(seed), 7)
    return {
        "tokens": centred(key_of[0], (HEIGHT, WIDTH, D), 1.0, 6.0, ((0, 8), (1, 32))),
        "cotangent": centred(key_of[1], (HEIGHT, WIDTH, D), 1.0, 6.0, ((0, 8), (1, 32))),
        "state_in": centred(key_of[2], (HEIGHT, WIDTH, N), 0.03125, 0.25, ((0, 8), (1, 32)), jnp.float32),
        "state_out": centred(key_of[3], (HEIGHT, WIDTH, N), 0.03125, 0.25, ((0, 8), (1, 32)), jnp.float32),
        "width_decay": draw_width_decay(jax.random.fold_in(key_of[6], 71), 0),
        "height_decay": draw_height_decay(jax.random.fold_in(key_of[6], 71), 0),
    }


def advance(carry, item):
    rate, term = item
    carry = rate * carry + term
    return carry, carry


def retreat(carry, item):
    rate, term = item
    total = term + carry
    return rate * total, total


def slab_grads(values, grads_out, log_width, log_height, state_in, state_out):
    width_rate = jnp.exp(log_width)[:, :, None, :]
    height_rate = jnp.exp(log_height)[:, :, None, :]
    slab_width = values.shape[2]
    driven = state_in[:, :, :, None] * values[:, :, None, :]
    zero_rows = jnp.zeros((HEIGHT, N, slab_width), jnp.float32)
    zero_cols = jnp.zeros((WIDTH, N, slab_width), jnp.float32)
    ignored, states = lax.scan(advance, zero_rows, (jnp.swapaxes(width_rate, 0, 1), jnp.swapaxes(driven, 0, 1)))
    states = jnp.swapaxes(states, 0, 1)
    ignored, totals = lax.scan(advance, zero_cols, (height_rate, states))
    seeded = state_out[:, :, :, None] * grads_out[:, :, None, :]
    ignored, col_grad = lax.scan(retreat, zero_cols, (height_rate, seeded), reverse=True)
    earlier_rows = jnp.concatenate([jnp.zeros_like(totals[:1]), totals[:-1]], axis=0)
    height_grad = jnp.exp(log_height) * jnp.sum(col_grad * earlier_rows, axis=2)
    out_grad = jnp.sum(totals * grads_out[:, :, None, :], axis=3)
    ignored, row_grad = lax.scan(retreat, zero_rows, (jnp.swapaxes(width_rate, 0, 1), jnp.swapaxes(col_grad, 0, 1)), reverse=True)
    row_grad = jnp.swapaxes(row_grad, 0, 1)
    earlier_cols = jnp.concatenate([jnp.zeros_like(states[:, :1]), states[:, :-1]], axis=1)
    width_grad = jnp.exp(log_width) * jnp.sum(row_grad * earlier_cols, axis=2)
    in_grad = jnp.sum(row_grad * values[:, :, None, :], axis=3)
    token_grad = jnp.sum(row_grad * state_in[:, :, :, None], axis=2)
    return token_grad, in_grad, out_grad, width_grad, height_grad


def reference(tokens, cotangent, state_in, state_out, width_decay, height_decay):
    slab_width = 8
    count = D // slab_width
    group_width = D // G

    def one_slab(carry, number):
        offset = (number * slab_width).astype(jnp.int32)
        values = lax.dynamic_slice_in_dim(tokens, offset, slab_width, 2).astype(jnp.float32)
        grads_out = lax.dynamic_slice_in_dim(cotangent, offset, slab_width, 2).astype(jnp.float32)
        group = (offset // group_width).astype(jnp.int32)
        log_width = jnp.broadcast_to(lax.dynamic_slice_in_dim(width_decay, group, 1, 2), (HEIGHT, WIDTH, slab_width))
        log_height = jnp.broadcast_to(lax.dynamic_slice_in_dim(height_decay, group, 1, 2), (HEIGHT, WIDTH, slab_width))
        token_grad, in_grad, out_grad, width_grad, height_grad = slab_grads(values, grads_out, log_width, log_height, state_in, state_out)
        return (carry[0] + in_grad, carry[1] + out_grad), (token_grad, jnp.sum(width_grad, axis=2), jnp.sum(height_grad, axis=2))

    start = (jnp.zeros((HEIGHT, WIDTH, N), jnp.float32), jnp.zeros((HEIGHT, WIDTH, N), jnp.float32))
    sums, slabs = lax.scan(one_slab, start, jnp.arange(count, dtype=jnp.int32))
    token_parts, width_parts, height_parts = slabs
    tokens_grad = jnp.transpose(token_parts, (1, 2, 0, 3)).reshape(HEIGHT, WIDTH, D)
    width_decay_grad = jnp.transpose(jnp.sum(width_parts.reshape(G, group_width // slab_width, HEIGHT, WIDTH), axis=1), (1, 2, 0))
    height_decay_grad = jnp.transpose(jnp.sum(height_parts.reshape(G, group_width // slab_width, HEIGHT, WIDTH), axis=1), (1, 2, 0))
    return tokens_grad, sums[0], sums[1], width_decay_grad, height_decay_grad
```

```python
import jax
import jax.numpy as jnp
from jax import lax
from jax.experimental import pallas as pl
from jax.experimental.pallas import tpu as pltpu
from jax.sharding import PartitionSpec as P

F32 = jnp.float32
BF16 = jnp.bfloat16

SEG = 8
ROWS = 8
COLS = 16
CH = 64
N = 16
LANES = SEG * N
STEP = 16

X0, C0, B0, S0, D0 = 0, 64, 128, 144, 160
SENT = 168
BACK = 104
EDGE = 40


def spread(ref, at, wide, place):
    for pair in range(ROWS // 2):
        block = ref[:, at + pair * COLS : at + (pair + 1) * COLS, :].reshape(SEG * COLS, 2 * CH)
        flipped = block.T.astype(BF16)
        for two in range(COLS // 2):
            out = jnp.dot(flipped, place[:, two * 256 : (two + 1) * 256], preferred_element_type=F32)
            for part in range(2):
                for half in range(2):
                    wide[2 * two + half, 2 * pair + part] = out[
                        part * CH : (part + 1) * CH, half * LANES : (half + 1) * LANES
                    ]


def make_place(place):
    k = lax.broadcasted_iota(jnp.int32, (LANES, 256), 0)
    m = lax.broadcasted_iota(jnp.int32, (LANES, 256), 1)
    for two in range(COLS // 2):
        col = 2 * two + m // LANES
        hit = k == ((m % LANES) // N) * COLS + col
        place[:, two * 256 : (two + 1) * 256] = jnp.where(hit, 1.0, 0.0).astype(BF16)


def small(ref, bt, ct, wr, hr):
    bt[...] = ref[:, B0 : B0 + N, :].reshape(LANES, 128).T.reshape(COLS, ROWS, LANES)
    ct[...] = ref[:, S0 : S0 + N, :].reshape(LANES, 128).T.reshape(COLS, ROWS, LANES)
    for row, out in ((D0, wr), (D0 + 1, hr)):
        rate = jnp.exp(ref[:, row : row + 1, :])
        wide = jnp.broadcast_to(rate, (SEG, N, 128)).reshape(LANES, 128)
        out[...] = wide.T.reshape(COLS, ROWS, LANES)


def carry_scan(ends, rates, down):
    lane = lax.broadcasted_iota(jnp.int32, (1, LANES), 1)
    keep = (lane >= N) if down else (lane < LANES - N)

    def move(v, by):
        return pltpu.roll(v, by * N if down else LANES - by * N, 1)

    one = jnp.where(keep, move(rates, 1), 0.0)
    two = one * move(one, 1)
    four = two * move(two, 2)

    def run(e):
        f = jnp.where(keep, move(e, 1), 0.0)
        f = f + one * move(f, 1)
        f = f + two * move(f, 2)
        return f + four * move(f, 4)

    return run(ends)


def segment_rate(hr, col):
    rate = hr[col, 0:1, :]
    for row in range(1, ROWS):
        rate = rate * hr[col, row : row + 1, :]
    return jnp.broadcast_to(rate, (ROWS, LANES))


def edges_kernel(ref, edge, back, place, xe, ce, bt, ct, wr, hr, tail, head):
    make_place(place)
    small(ref, bt, ct, wr, hr)
    spread(ref, X0, xe, place)
    spread(ref, C0, ce, place)

    def ends(col, keep):
        rate = segment_rate(hr, col)[0:1]
        for c in range(0, CH, STEP):
            carry = jnp.zeros((STEP, LANES), F32)
            for row in reversed(range(ROWS)):
                carry = hr[col, row : row + 1, :] * (
                    carry + ct[col, row : row + 1, :] * ce[col, row, c : c + STEP, :]
                )
            back[col, c : c + STEP, :] = carry_scan(carry, rate, False)
        return keep

    lax.fori_loop(0, COLS, ends, 0)
    tail[...] = jnp.zeros_like(tail)
    head[...] = jnp.zeros_like(head)

    def sums(step, after):
        col = COLS - 1 - step
        weights = [after[r] * bt[col, r : r + 1, :] for r in range(ROWS)]
        for c in range(0, CH, STEP):
            carry = back[col, c : c + STEP, :]
            for row in reversed(range(ROWS)):
                grad = carry + ct[col, row : row + 1, :] * ce[col, row, c : c + STEP, :]
                carry = hr[col, row : row + 1, :] * grad
                head[row, c : c + STEP, :] = wr[col, row : row + 1, :] * (
                    head[row, c : c + STEP, :] + grad
                )
                tail[row, c : c + STEP, :] += weights[row] * xe[col, row, c : c + STEP, :]
        return tuple(after[r] * wr[col, r : r + 1, :] for r in range(ROWS))

    total = lax.fori_loop(0, COLS, sums, tuple(jnp.ones((1, LANES), F32) for r in range(ROWS)))
    for row in range(ROWS):
        for q in range(CH // STEP):
            at = row * (CH // STEP) + q
            edge[at, 0:STEP, :] = tail[row, q * STEP : (q + 1) * STEP, :]
            edge[at, STEP : 2 * STEP, :] = head[row, q * STEP : (q + 1) * STEP, :]
            edge[at, 2 * STEP :, :] = jnp.broadcast_to(total[row], (EDGE - 2 * STEP, LANES))


def chain_kernel(got, out):
    count = got.shape[0]

    def right(place, carry):
        out[place, 0:STEP, :] = carry
        return got[place, 2 * STEP : 2 * STEP + 1, :] * carry + got[place, 0:STEP, :]

    def left(hop, carry):
        place = count - 1 - hop
        out[place, STEP : 2 * STEP, :] = carry
        return got[place, 2 * STEP : 2 * STEP + 1, :] * carry + got[place, STEP : 2 * STEP, :]

    def both(hop, carry):
        return right(hop, carry[0]), left(hop, carry[1])

    zero = jnp.zeros((STEP, LANES), F32)
    lax.fori_loop(0, count, both, (zero, zero), unroll=4)


def grads_kernel(
    ref, edge, back, out, place, xe, ce, bt, ct, wr, hr, states, front, run, pieces, gather, sums, acc
):
    make_place(place)
    small(ref, bt, ct, wr, hr)
    spread(ref, X0, xe, place)
    spread(ref, C0, ce, place)
    k = lax.broadcasted_iota(jnp.int32, (2 * LANES, 128), 0)
    m = lax.broadcasted_iota(jnp.int32, (2 * LANES, 128), 1)
    for col in range(COLS):
        gather[col] = jnp.where(m == ((k % LANES) // N) * COLS + col, 1.0, 0.0).astype(BF16)
    for row in range(ROWS):
        for q in range(CH // STEP):
            at = row * (CH // STEP) + q
            states[0, row, q * STEP : (q + 1) * STEP, :] = edge[at, 0:STEP, :]
            run[row, q * STEP : (q + 1) * STEP, :] = edge[at, STEP : 2 * STEP, :]

    def forward(col, keep):
        rate = segment_rate(hr, col)[0:1]
        for c in range(0, CH, STEP):
            total = jnp.zeros((STEP, LANES), F32)
            for row in range(ROWS):
                state = (
                    wr[col, row : row + 1, :] * states[col, row, c : c + STEP, :]
                    + bt[col, row : row + 1, :] * xe[col, row, c : c + STEP, :]
                )
                states[col + 1, row, c : c + STEP, :] = state
                total = hr[col, row : row + 1, :] * total + state
            front[col, c : c + STEP, :] = carry_scan(total, rate, True)
        return keep

    lax.fori_loop(0, COLS, forward, 0)

    def fold(v):
        return v[0:8] + v[8:16]

    def products(step, keep):
        col = COLS - 1 - step
        in_sum = [jnp.zeros((8, LANES), F32) for r in range(ROWS)]
        out_sum = [jnp.zeros((8, LANES), F32) for r in range(ROWS)]
        w_sum = [jnp.zeros((8, LANES), F32) for r in range(ROWS)]
        h_sum = [jnp.zeros((8, LANES), F32) for r in range(ROWS)]
        for c in range(0, CH, STEP):
            carry = back[col, c : c + STEP, :]
            grads = [None] * ROWS
            for row in reversed(range(ROWS)):
                grads[row] = carry + ct[col, row : row + 1, :] * ce[col, row, c : c + STEP, :]
                carry = hr[col, row : row + 1, :] * grads[row]
            total = front[col, c : c + STEP, :]
            for row in range(ROWS):
                h_sum[row] = h_sum[row] + fold(grads[row] * total)
                total = hr[col, row : row + 1, :] * total + states[col + 1, row, c : c + STEP, :]
                out_sum[row] = out_sum[row] + fold(total * ce[col, row, c : c + STEP, :])
                grad = grads[row] + run[row, c : c + STEP, :]
                run[row, c : c + STEP, :] = wr[col, row : row + 1, :] * grad
                w_sum[row] = w_sum[row] + fold(grad * states[col, row, c : c + STEP, :])
                in_sum[row] = in_sum[row] + fold(grad * xe[col, row, c : c + STEP, :])
                piece = grad * bt[col, row : row + 1, :]
                high = piece.astype(BF16)
                pieces[col, row * CH + c : row * CH + c + STEP, 0:LANES] = high
                pieces[col, row * CH + c : row * CH + c + STEP, LANES:] = (
                    piece - high.astype(F32)
                ).astype(BF16)
        for row in range(ROWS):
            for which, value in enumerate((in_sum, out_sum, w_sum, h_sum)):
                sums[which, col, row : row + 1, :] = jnp.sum(value[row], axis=0, keepdims=True)
        return keep

    lax.fori_loop(0, COLS, products, 0)
    acc[...] = jnp.zeros_like(acc)

    def collect(col, keep):
        acc[...] += jnp.dot(pieces[col], gather[col], preferred_element_type=F32)
        return keep

    lax.fori_loop(0, COLS, collect, 0)
    for pair in range(ROWS // 2):
        block = acc[pair * 2 * CH : (pair + 1) * 2 * CH, :].T
        out[:, pair * COLS : (pair + 1) * COLS, :] = block.reshape(SEG, COLS, 2 * CH)
    for which in range(2):
        flat = sums[which].reshape(COLS * ROWS, LANES).T
        out[:, 64 + which * N : 64 + (which + 1) * N, :] = flat.reshape(SEG, N, COLS * ROWS)
    for which in range(2):
        flat = sums[2 + which].reshape(COLS * ROWS, LANES).T.reshape(SEG, N, COLS * ROWS)
        rate = jnp.exp(ref[:, D0 + which : D0 + which + 1, :])
        out[:, 96 + which : 97 + which, :] = rate * jnp.sum(flat, axis=1, keepdims=True)
    out[:, 98:, :] = jnp.zeros((SEG, BACK - 98, 128), F32)


WIDE = (COLS, ROWS, CH, LANES)
TOKEN = (COLS, ROWS, LANES)


def vm(shape, kind=F32):
    return pltpu.VMEM(shape, kind)


PARAMS = pltpu.CompilerParams(vmem_limit_bytes=56 * 1024 * 1024)


def per_device(tokens, cotangent, state_in, state_out, width_decay, height_decay):
    def by_group(a):
        a = a.astype(F32).reshape(ROWS // 2, 2, COLS, SEG, CH)
        return jnp.transpose(a, (3, 0, 2, 1, 4)).reshape(SEG, 64, 128)

    def to_all(a):
        flat = jnp.transpose(a, (2, 1, 0)).reshape(1, N, COLS * ROWS)
        return jnp.broadcast_to(flat, (SEG, N, COLS * ROWS))

    def decay(a):
        return jnp.transpose(a, (2, 1, 0)).reshape(SEG, 1, COLS * ROWS)

    message = jnp.concatenate(
        [
            by_group(tokens),
            by_group(cotangent),
            to_all(state_in),
            to_all(state_out),
            decay(width_decay),
            decay(height_decay),
            jnp.zeros((SEG, SENT - 162, 128), F32),
        ],
        axis=1,
    )
    tile = lax.all_to_all(message, "ha", 0, 0, tiled=True)
    devices = lax.axis_size("wa")
    base = [vm((128, 2048), BF16), vm(WIDE), vm(WIDE), vm(TOKEN), vm(TOKEN), vm(TOKEN), vm(TOKEN)]
    edge, back = pl.pallas_call(
        edges_kernel,
        out_shape=(
            jax.ShapeDtypeStruct((devices, EDGE, LANES), F32),
            jax.ShapeDtypeStruct((COLS, CH, LANES), F32),
        ),
        scratch_shapes=base + [vm((ROWS, CH, LANES)), vm((ROWS, CH, LANES))],
        compiler_params=PARAMS,
    )(tile)
    edge = lax.all_to_all(edge, "wa", 0, 0, tiled=True)
    carries = pl.pallas_call(
        chain_kernel,
        out_shape=jax.ShapeDtypeStruct((devices, 2 * STEP, LANES), F32),
        compiler_params=PARAMS,
    )(edge)
    carries = lax.all_to_all(carries, "wa", 0, 0, tiled=True)
    grads = pl.pallas_call(
        grads_kernel,
        out_shape=jax.ShapeDtypeStruct((SEG, BACK, 128), F32),
        scratch_shapes=base
        + [
            vm((COLS + 1,) + WIDE[1:]),
            vm((COLS, CH, LANES)),
            vm((ROWS, CH, LANES)),
            vm((COLS, ROWS * CH, 2 * LANES), BF16),
            vm((COLS, 2 * LANES, 128), BF16),
            vm((4,) + TOKEN),
            vm((ROWS * CH, 128)),
        ],
        compiler_params=PARAMS,
    )(tile, carries, back)
    grads = lax.all_to_all(grads, "ha", 0, 0, tiled=True)
    tokens_grad = grads[:, :64].reshape(SEG, ROWS // 2, COLS, 2, CH)
    tokens_grad = jnp.transpose(tokens_grad, (1, 3, 2, 0, 4)).reshape(ROWS, COLS, SEG * CH)

    def summed(a):
        return jnp.transpose(jnp.sum(a, axis=0).reshape(N, COLS, ROWS), (2, 1, 0))

    def decays(a):
        return jnp.transpose(a.reshape(SEG, COLS, ROWS), (2, 1, 0))

    return (
        tokens_grad,
        summed(grads[:, 64:80]),
        summed(grads[:, 80:96]),
        decays(grads[:, 96]),
        decays(grads[:, 97]),
    )


def solution(mesh):
    spec = P("ha", "wa", None)
    return jax.shard_map(
        per_device, mesh=mesh, in_specs=(spec,) * 6, out_specs=(spec,) * 5, check_vma=False
    )
```

```python
import jax
import jax.numpy as jnp
from jax import lax
from jax.experimental import pallas as pl
from jax.experimental.pallas import tpu as pltpu
from jax.sharding import PartitionSpec as P

F32 = jnp.float32
BF16 = jnp.bfloat16

SEG = 8
ROWS = 8
COLS = 16
CH = 64
N = 16
LANES = SEG * N
TOKENS = ROWS * COLS
STEP = 16
QUART = CH // STEP

X0, C0, B0, S0, D0 = 0, 64, 128, 144, 160
SENT = 168
I0, O0, W0 = 64, 80, 96
BACK = 104
EDGE = 40


def pack_kernel(x, y, b, s, w, h, out):
    low = lax.broadcasted_iota(jnp.int32, (COLS, 128), 1) < CH
    for at, a in ((X0, x), (C0, y)):
        for pair in range(ROWS // 2):
            rows = slice(at + pair * COLS, at + (pair + 1) * COLS)
            for two in range(SEG // 2):
                lanes = slice(two * 128, (two + 1) * 128)
                one = a[2 * pair, :, lanes].astype(F32)
                other = a[2 * pair + 1, :, lanes].astype(F32)
                out[2 * two, rows, :] = jnp.where(low, one, pltpu.roll(other, CH, 1))
                out[2 * two + 1, rows, :] = jnp.where(low, pltpu.roll(one, CH, 1), other)
    for at, a in ((B0, b), (S0, s)):
        flat = a[...].reshape(TOKENS, N).T
        for g in range(SEG):
            out[g, at : at + N, :] = flat
    for at, a in ((D0, w), (D0 + 1, h)):
        flat = a[...].reshape(TOKENS, SEG).T
        for g in range(SEG):
            out[g, at : at + 1, :] = flat[g : g + 1]
    out[:, D0 + 2 :, :] = jnp.zeros((SEG, SENT - D0 - 2, 128), F32)


def unpack_kernel(got, x, b, s, w, h):
    low = lax.broadcasted_iota(jnp.int32, (COLS, 128), 1) < CH
    for pair in range(ROWS // 2):
        rows = slice(pair * COLS, (pair + 1) * COLS)
        for two in range(SEG // 2):
            lanes = slice(two * 128, (two + 1) * 128)
            one = got[2 * two, rows, :]
            other = got[2 * two + 1, rows, :]
            x[2 * pair, :, lanes] = jnp.where(low, one, pltpu.roll(other, CH, 1))
            x[2 * pair + 1, :, lanes] = jnp.where(low, pltpu.roll(one, CH, 1), other)
    for at, a in ((I0, b), (O0, s)):
        flat = got[0, at : at + N, :]
        for g in range(1, SEG):
            flat = flat + got[g, at : at + N, :]
        a[...] = flat.T.reshape(ROWS, COLS, N)
    for at, a in ((W0, w), (W0 + 1, h)):
        flat = jnp.concatenate([got[g, at : at + 1, :] for g in range(SEG)], axis=0)
        a[...] = flat.T.reshape(ROWS, COLS, SEG)


def make_place(place):
    k = lax.broadcasted_iota(jnp.int32, (LANES, 256), 0)
    m = lax.broadcasted_iota(jnp.int32, (LANES, 256), 1)
    for two in range(COLS // 2):
        col = 2 * two + m // LANES
        hit = k == ((m % LANES) // N) * COLS + col
        place[:, two * 256 : (two + 1) * 256] = jnp.where(hit, 1.0, 0.0).astype(BF16)


def flipped(ref, at, pair):
    block = ref[:, at + pair * COLS : at + (pair + 1) * COLS, :].reshape(SEG * COLS, 2 * CH)
    return block.T.astype(BF16)


def spread(ref, at, wide, place):
    for pair in range(ROWS // 2):
        block = flipped(ref, at, pair)
        for two in range(COLS // 2):
            out = jnp.dot(block, place[:, two * 256 : (two + 1) * 256], preferred_element_type=F32)
            for part in range(2):
                for half in range(2):
                    wide[2 * two + half, 2 * pair + part] = out[
                        part * CH : (part + 1) * CH, half * LANES : (half + 1) * LANES
                    ]


def by_column(flat, out):
    for col in range(COLS):
        out[col] = flat[pl.ds(col, ROWS, stride=COLS), :]


def small(ref, flat, bt, ct, wr, hr):
    for at, out in ((B0, bt), (S0, ct)):
        flat[...] = ref[:, at : at + N, :].reshape(LANES, TOKENS).T
        by_column(flat, out)
    for at, out in ((D0, wr), (D0 + 1, hr)):
        rate = jnp.exp(ref[:, at : at + 1, :])
        flat[...] = jnp.broadcast_to(rate, (SEG, N, TOKENS)).reshape(LANES, TOKENS).T
        by_column(flat, out)


def mover(down):
    def move(v, by):
        return pltpu.roll(v, by * N if down else LANES - by * N, 1)

    return move


def inside(down):
    lane = lax.broadcasted_iota(jnp.int32, (1, LANES), 1)
    return (lane >= N) if down else (lane < LANES - N)


def carry_rates(flat, rates, down):
    move = mover(down)
    total = flat[0:COLS, :]
    for row in range(1, ROWS):
        total = total * flat[row * COLS : (row + 1) * COLS, :]
    one = jnp.where(inside(down), move(total, 1), 0.0)
    two = one * move(one, 1)
    rates[0] = one
    rates[1] = two
    rates[2] = two * move(two, 2)


def carry_scan(ends, rates, down):
    move = mover(down)
    keep = inside(down)

    def column(col, none):
        f = jnp.where(keep, move(ends[col], 1), 0.0)
        for k, by in enumerate((1, 2, 4)):
            f = f + rates[k, pl.ds(col, 1), :] * move(f, by)
        ends[col] = f
        return none

    lax.fori_loop(0, COLS, column, 0, unroll=4)


def split(v):
    high = v.astype(BF16)
    return high, (v - high.astype(F32)).astype(BF16)


def edges_kernel(ref, edge, back, place, ce, bt, ct, wr, hr, flat, rates, head):
    make_place(place)
    small(ref, flat, bt, ct, wr, hr)
    carry_rates(flat, rates, False)
    spread(ref, C0, ce, place)

    def ends(col, none):
        carry = jnp.zeros((CH, LANES), F32)
        for row in reversed(range(ROWS)):
            one = slice(row, row + 1)
            carry = hr[col, one, :] * (carry + ct[col, one, :] * ce[col, row])
        back[col] = carry
        return none

    lax.fori_loop(0, COLS, ends, 0, unroll=2)
    carry_scan(back, rates, False)

    after = jnp.ones((ROWS, LANES), F32)
    for col in reversed(range(COLS)):
        flat[col * ROWS : (col + 1) * ROWS, :] = after * bt[col]
        after = after * wr[col]
    r = lax.broadcasted_iota(jnp.int32, (LANES, LANES), 0)
    m = lax.broadcasted_iota(jnp.int32, (LANES, LANES), 1)
    own = r // COLS == m // N
    for pair in range(ROWS // 2):
        block = flipped(ref, X0, pair)
        for part in range(2):
            row = 2 * pair + part
            weight = flat[pl.ds(row, COLS, stride=ROWS), :]
            weight = jnp.where(own, jnp.concatenate([weight] * SEG, axis=0), 0.0)
            high, low = split(weight)
            mine = block[part * CH : (part + 1) * CH]
            tail = jnp.dot(mine, high, preferred_element_type=F32) + jnp.dot(
                mine, low, preferred_element_type=F32
            )
            for q in range(QUART):
                edge[row * QUART + q, 0:STEP, :] = tail[q * STEP : (q + 1) * STEP]
                edge[row * QUART + q, 2 * STEP :, :] = jnp.broadcast_to(
                    after[row : row + 1], (EDGE - 2 * STEP, LANES)
                )

    head[...] = jnp.zeros_like(head)

    def sums(step, none):
        col = COLS - 1 - 2 * step
        carry, carry2 = back[col], back[col - 1]
        for row in reversed(range(ROWS)):
            one = slice(row, row + 1)
            grad = carry + ct[col, one, :] * ce[col, row]
            carry = hr[col, one, :] * grad
            grad2 = carry2 + ct[col - 1, one, :] * ce[col - 1, row]
            carry2 = hr[col - 1, one, :] * grad2
            head[row] = wr[col - 1, one, :] * (wr[col, one, :] * (head[row] + grad) + grad2)
        return none

    lax.fori_loop(0, COLS // 2, sums, 0)
    for row in range(ROWS):
        for q in range(QUART):
            edge[row * QUART + q, STEP : 2 * STEP, :] = head[row, q * STEP : (q + 1) * STEP, :]


def chain_kernel(got, out):
    count = got.shape[0]

    def both(hop, carry):
        right, left = carry
        place = count - 1 - hop
        out[hop, 0:STEP, :] = right
        out[place, STEP : 2 * STEP, :] = left
        right = got[hop, 2 * STEP : 2 * STEP + 1, :] * right + got[hop, 0:STEP, :]
        left = got[place, 2 * STEP : 2 * STEP + 1, :] * left + got[place, STEP : 2 * STEP, :]
        return right, left

    zero = jnp.zeros((STEP, LANES), F32)
    lax.fori_loop(0, count, both, (zero, zero), unroll=8)


def total8(v):
    v = v[0 : CH // 2] + v[CH // 2 :]
    v = v[0 : CH // 4] + v[CH // 4 :]
    return v[0:8] + v[8:16]


def grads_kernel(
    ref, edge, back, out, place, xe, ce, bt, ct, wr, hr, flat, rates, states, front, run, kept, pieces, gather, sums
):
    make_place(place)
    small(ref, flat, bt, ct, wr, hr)
    carry_rates(flat, rates, True)
    spread(ref, X0, xe, place)
    spread(ref, C0, ce, place)
    k = lax.broadcasted_iota(jnp.int32, (2 * LANES, 128), 0)
    m = lax.broadcasted_iota(jnp.int32, (2 * LANES, 128), 1)
    for col in range(COLS):
        gather[col * 2 * LANES : (col + 1) * 2 * LANES, :] = jnp.where(
            m == ((k % LANES) // N) * COLS + col, 1.0, 0.0
        ).astype(BF16)
    for row in range(ROWS):
        for q in range(QUART):
            part = slice(q * STEP, (q + 1) * STEP)
            states[0, row, part, :] = edge[row * QUART + q, 0:STEP, :]
            run[row, part, :] = edge[row * QUART + q, STEP : 2 * STEP, :]

    def forward(col, none):
        total = jnp.zeros((CH, LANES), F32)
        for row in range(ROWS):
            one = slice(row, row + 1)
            state = wr[col, one, :] * states[col, row] + bt[col, one, :] * xe[col, row]
            states[col + 1, row] = state
            total = hr[col, one, :] * total + state
        front[col] = total
        return none

    lax.fori_loop(0, COLS, forward, 0)
    carry_scan(front, rates, True)

    def products(step, none):
        col = COLS - 1 - step
        carry = back[col]
        for row in reversed(range(ROWS)):
            one = slice(row, row + 1)
            grad = carry + ct[col, one, :] * ce[col, row]
            carry = hr[col, one, :] * grad
            kept[row] = grad
        total = front[col]
        for row in range(ROWS):
            one = slice(row, row + 1)
            grad = kept[row]
            sums[3, row, col] = total8(grad * total)
            total = hr[col, one, :] * total + states[col + 1, row]
            sums[1, row, col] = total8(total * ce[col, row])
            grad = grad + run[row]
            run[row] = wr[col, one, :] * grad
            sums[2, row, col] = total8(grad * states[col, row])
            sums[0, row, col] = total8(grad * xe[col, row])
            high, low = split(grad * bt[col, one, :])
            pieces[col, row * CH : (row + 1) * CH, 0:LANES] = high
            pieces[col, row * CH : (row + 1) * CH, LANES:] = low
        return none

    lax.fori_loop(0, COLS, products, 0)
    for pair in range(ROWS // 2):
        rows = slice(pair * 2 * CH, (pair + 1) * 2 * CH)
        block = jnp.zeros((2 * CH, 128), F32)
        for col in range(COLS):
            block = block + jnp.dot(
                pieces[col, rows, :], gather[col * 2 * LANES : (col + 1) * 2 * LANES, :], preferred_element_type=F32
            )
        out[:, pair * COLS : (pair + 1) * COLS, :] = block.T.reshape(SEG, COLS, 2 * CH)
    for which, at in enumerate((I0, O0, W0, W0 + 1)):
        rows = sums.at[which].reshape(TOKENS * 8, LANES)
        value = rows[pl.ds(0, TOKENS, stride=8), :]
        for k in range(1, 8):
            value = value + rows[pl.ds(k, TOKENS, stride=8), :]
        value = value.T.reshape(SEG, N, TOKENS)
        if which < 2:
            out[:, at : at + N, :] = value
        else:
            rate = jnp.exp(ref[:, D0 + which - 2 : D0 + which - 1, :])
            out[:, at : at + 1, :] = rate * jnp.sum(value, axis=1, keepdims=True)
    out[:, W0 + 2 :, :] = jnp.zeros((SEG, BACK - W0 - 2, 128), F32)


WIDE = (COLS, ROWS, CH, LANES)
TOKEN = (COLS, ROWS, LANES)


def vm(shape, kind=F32):
    return pltpu.VMEM(shape, kind)


def call(kernel, ins, outs, scratch, mebibytes):
    whole = pl.BlockSpec(memory_space=pltpu.VMEM)
    shapes = tuple(jax.ShapeDtypeStruct(s, F32) for s in outs)
    single = len(outs) == 1
    return pl.pallas_call(
        kernel,
        out_shape=shapes[0] if single else shapes,
        in_specs=[whole] * ins,
        out_specs=whole if single else (whole,) * len(outs),
        scratch_shapes=scratch,
        compiler_params=pltpu.CompilerParams(vmem_limit_bytes=mebibytes * 1024 * 1024),
    )


SMALL = [vm(TOKEN)] * 4 + [vm((TOKENS, LANES)), vm((3, COLS, LANES))]
PLACE = vm((128, 2048), BF16)


def packs():
    return call(pack_kernel, 6, [(SEG, SENT, 128)], [], 8)


def edges(devices):
    outs = [(devices, EDGE, LANES), (COLS, CH, LANES)]
    return call(edges_kernel, 1, outs, [PLACE, vm(WIDE)] + SMALL + [vm((ROWS, CH, LANES))], 16)


def chains(devices):
    return call(chain_kernel, 1, [(devices, 2 * STEP, LANES)], [], 8)


def grads():
    block = (ROWS, CH, LANES)
    scratch = [PLACE, vm(WIDE), vm(WIDE)] + SMALL
    scratch += [vm((COLS + 1,) + block), vm((COLS, CH, LANES)), vm(block), vm(block)]
    scratch += [
        vm((COLS, ROWS * CH, 2 * LANES), BF16),
        vm((COLS * 2 * LANES, 128), BF16),
        vm((4, ROWS, COLS, 8, LANES)),
    ]
    return call(grads_kernel, 3, [(SEG, BACK, 128)], scratch, 32)


def unpacks():
    outs = [(ROWS, COLS, SEG * CH)] + [(ROWS, COLS, N)] * 2 + [(ROWS, COLS, SEG)] * 2
    return call(unpack_kernel, 1, outs, [], 8)


def per_device(*arrays):
    devices = lax.axis_size("wa")
    tile = lax.all_to_all(packs()(*arrays), "ha", 0, 0, tiled=True)
    edge, back = edges(devices)(tile)
    edge = lax.all_to_all(edge, "wa", 0, 0, tiled=True)
    carries = lax.all_to_all(chains(devices)(edge), "wa", 0, 0, tiled=True)
    answer = grads()(tile, carries, back)
    return unpacks()(lax.all_to_all(answer, "ha", 0, 0, tiled=True))


def solution(mesh):
    spec = P("ha", "wa", None)
    return jax.shard_map(
        per_device, mesh=mesh, in_specs=(spec,) * 6, out_specs=(spec,) * 5, check_vma=False
    )
```

```python
import jax
import jax.numpy as jnp
from jax import lax
from jax.experimental import pallas as pl
from jax.experimental.pallas import tpu as pltpu
from jax.sharding import PartitionSpec as P

F32 = jnp.float32
BF16 = jnp.bfloat16

SEG = 8
ROWS = 8
COLS = 16
CH = 64
N = 16
LANES = SEG * N
TOKENS = ROWS * COLS
STEP = 16
QUART = CH // STEP

X0, C0, B0, S0, D0 = 0, 64, 128, 144, 160
SENT = 168
I0, O0, W0 = 64, 80, 96
BACK = 104
EDGE = 40
UE, US, UF, UP = 2, 1, 1, 1
PK = 60


def make_place(place):
    k = lax.broadcasted_iota(jnp.int32, (LANES, 256), 0)
    m = lax.broadcasted_iota(jnp.int32, (LANES, 256), 1)
    for two in range(COLS // 2):
        col = 2 * two + m // LANES
        hit = k == ((m % LANES) // N) * COLS + col
        place[two] = jnp.where(hit, 1.0, 0.0).astype(BF16)


def make_gather(gather):
    k = lax.broadcasted_iota(jnp.int32, (2 * LANES, 128), 0)
    m = lax.broadcasted_iota(jnp.int32, (2 * LANES, 128), 1)
    for col in range(COLS):
        hit = m == ((k % LANES) // N) * COLS + col
        gather[col] = jnp.where(hit, 1.0, 0.0).astype(BF16)


def pack_kernel(x0, y0, b0, s0, w0, h0, out, x, y, b, s, w, h, done):
    copies = [
        pltpu.make_async_copy(source, target, done.at[k])
        for k, (source, target) in enumerate(((w0, w), (h0, h), (b0, b), (s0, s), (x0, x), (y0, y)))
    ]
    for copy in copies:
        copy.start()
    low = lax.broadcasted_iota(jnp.int32, (COLS, 128), 1) < CH
    out[:, D0 + 2 :, :] = jnp.zeros((SEG, SENT - D0 - 2, 128), F32)
    for k, (at, a) in enumerate(((D0, w), (D0 + 1, h))):
        copies[k].wait()
        flat = jnp.concatenate([a[row] for row in range(ROWS)], axis=1)
        for g in range(SEG):
            out[g, at : at + 1, :] = flat[g : g + 1]
    for k, (at, a) in enumerate(((B0, b), (S0, s))):
        copies[2 + k].wait()
        flat = a[...].reshape(TOKENS, N).T
        for g in range(SEG):
            out[g, at : at + N, :] = flat
    for k, (at, a) in enumerate(((X0, x), (C0, y))):
        copies[4 + k].wait()
        for pair in range(ROWS // 2):
            rows = slice(at + pair * COLS, at + (pair + 1) * COLS)
            for two in range(SEG // 2):
                lanes = slice(two * 128, (two + 1) * 128)
                one = a[2 * pair, :, lanes].astype(F32)
                other = a[2 * pair + 1, :, lanes].astype(F32)
                out[2 * two, rows, :] = jnp.where(low, one, pltpu.roll(other, CH, 1))
                out[2 * two + 1, rows, :] = jnp.where(low, pltpu.roll(one, CH, 1), other)


def unpack_kernel(got, x, b, s, w, h):
    low = lax.broadcasted_iota(jnp.int32, (COLS, 128), 1) < CH
    for pair in range(ROWS // 2):
        rows = slice(pair * COLS, (pair + 1) * COLS)
        for two in range(SEG // 2):
            lanes = slice(two * 128, (two + 1) * 128)
            one = got[2 * two, rows, :]
            other = got[2 * two + 1, rows, :]
            x[2 * pair, :, lanes] = jnp.where(low, one, pltpu.roll(other, CH, 1))
            x[2 * pair + 1, :, lanes] = jnp.where(low, pltpu.roll(one, CH, 1), other)
    for at, a in ((I0, b), (O0, s)):
        flat = got[0, at : at + N, :]
        for g in range(1, SEG):
            flat = flat + got[g, at : at + N, :]
        a[...] = flat.T.reshape(ROWS, COLS, N)
    for at, a in ((W0, w), (W0 + 1, h)):
        flat = jnp.concatenate([got[g, at : at + 1, :] for g in range(SEG)], axis=0)
        for row in range(ROWS):
            a[row] = flat[:, row * COLS : (row + 1) * COLS]


def flip(ref, at, flipped):
    for pair in range(ROWS // 2):
        block = ref[:, at + pair * COLS : at + (pair + 1) * COLS, :].reshape(SEG * COLS, 2 * CH)
        flipped[pair * 2 * CH : (pair + 1) * 2 * CH, :] = block.T.astype(BF16)


def spread(flipped, place, wide, two):
    for pair in range(ROWS // 2):
        block = flipped[pair * 2 * CH : (pair + 1) * 2 * CH, :]
        out = jnp.dot(block, place[two], preferred_element_type=F32)
        for part in range(2):
            for half in range(2):
                wide[2 * two + half, 2 * pair + part] = out[
                    part * CH : (part + 1) * CH, half * LANES : (half + 1) * LANES
                ]


def by_column(flat, out):
    for col in range(COLS):
        out[col] = flat[pl.ds(col, ROWS, stride=COLS), :]


def small(ref, flat, bt, ct, wr, hr):
    for at, out in ((B0, bt), (S0, ct)):
        flat[...] = ref[:, at : at + N, :].reshape(LANES, TOKENS).T
        by_column(flat, out)
    for at, out in ((D0, wr), (D0 + 1, hr)):
        rate = jnp.exp(ref[:, at : at + 1, :])
        flat[...] = jnp.broadcast_to(rate, (SEG, N, TOKENS)).reshape(LANES, TOKENS).T
        by_column(flat, out)


def tables(rows):
    return [rows.at[:, k * ROWS : (k + 1) * ROWS, :] for k in range(5)]


def mover(down):
    def move(v, by):
        return pltpu.roll(v, by * N if down else LANES - by * N, 1)

    return move


def inside(down):
    lane = lax.broadcasted_iota(jnp.int32, (1, LANES), 1)
    return (lane >= N) if down else (lane < LANES - N)


def carry_rates(flat, rates, down):
    move = mover(down)
    total = flat[0:COLS, :]
    for row in range(1, ROWS):
        total = total * flat[row * COLS : (row + 1) * COLS, :]
    one = jnp.where(inside(down), move(total, 1), 0.0)
    two = one * move(one, 1)
    rates[:, 0, :] = one
    rates[:, 1, :] = two
    rates[:, 2, :] = two * move(two, 2)


def carry_scan(ends, rates, down):
    move = mover(down)
    keep = inside(down)

    def column(col, none):
        f = jnp.where(keep, move(ends[col], 1), 0.0)
        for k, by in enumerate((1, 2, 4)):
            f = f + rates[col, k : k + 1, :] * move(f, by)
        ends[col] = f
        return none

    lax.fori_loop(0, COLS, column, 0, unroll=4)


def split(v):
    high = v.astype(BF16)
    return high, (v - high.astype(F32)).astype(BF16)


def own_segment():
    r = lax.broadcasted_iota(jnp.int32, (LANES, LANES), 0)
    m = lax.broadcasted_iota(jnp.int32, (LANES, LANES), 1)
    return r // COLS == m // N


def diagonal(flat, row, own):
    value = flat[pl.ds(row, COLS, stride=ROWS), :]
    return jnp.where(own, jnp.concatenate([value] * SEG, axis=0), 0.0)


def edges_kernel(ref, edge, back, rows, place, ce, flat, rates, head, flipped):
    make_place(place)
    bt, ct, wr, hr, down = tables(rows)
    small(ref, flat, bt, ct, wr, hr)
    carry_rates(flat, rates, False)
    carry_rates(flat, down, True)
    flip(ref, C0, flipped)
    for two in range(COLS // 2):
        spread(flipped, place, ce, two)

    def ends(col, none):
        carry = jnp.zeros((CH, LANES), F32)
        for row in reversed(range(ROWS)):
            one = slice(row, row + 1)
            carry = hr[col, one, :] * (carry + ct[col, one, :] * ce[col, row])
        back[col] = carry
        return none

    lax.fori_loop(0, COLS, ends, 0, unroll=UE)
    carry_scan(back, rates, False)

    after = jnp.ones((ROWS, LANES), F32)
    for col in reversed(range(COLS)):
        flat[col * ROWS : (col + 1) * ROWS, :] = after * bt[col]
        after = after * wr[col]
    own = own_segment()
    flip(ref, X0, flipped)
    for pair in range(ROWS // 2):
        for part in range(2):
            row = 2 * pair + part
            high, low = split(diagonal(flat, row, own))
            mine = flipped[row * CH : (row + 1) * CH, :]
            tail = jnp.dot(mine, high, preferred_element_type=F32) + jnp.dot(
                mine, low, preferred_element_type=F32
            )
            for q in range(QUART):
                edge[row * QUART + q, 0:STEP, :] = tail[q * STEP : (q + 1) * STEP]
                edge[row * QUART + q, 2 * STEP :, :] = jnp.broadcast_to(
                    after[row : row + 1], (EDGE - 2 * STEP, LANES)
                )

    head[...] = jnp.zeros_like(head)

    def sums(step, none):
        col = COLS - 1 - 2 * step
        carry, carry2 = back[col], back[col - 1]
        for row in reversed(range(ROWS)):
            one = slice(row, row + 1)
            grad = carry + ct[col, one, :] * ce[col, row]
            carry = hr[col, one, :] * grad
            grad2 = carry2 + ct[col - 1, one, :] * ce[col - 1, row]
            carry2 = hr[col - 1, one, :] * grad2
            head[row] = wr[col - 1, one, :] * (wr[col, one, :] * (head[row] + grad) + grad2)
        return none

    lax.fori_loop(0, COLS // 2, sums, 0, unroll=US)
    for row in range(ROWS):
        for q in range(QUART):
            edge[row * QUART + q, STEP : 2 * STEP, :] = head[row, q * STEP : (q + 1) * STEP, :]


def chain_kernel(got, out):
    count = got.shape[0]

    def both(hop, carry):
        right, left = carry
        place = count - 1 - hop
        out[hop, 0:STEP, :] = right
        out[place, STEP : 2 * STEP, :] = left
        right = got[hop, 2 * STEP : 2 * STEP + 1, :] * right + got[hop, 0:STEP, :]
        left = got[place, 2 * STEP : 2 * STEP + 1, :] * left + got[place, STEP : 2 * STEP, :]
        return right, left

    zero = jnp.zeros((STEP, LANES), F32)
    lax.fori_loop(0, count, both, (zero, zero), unroll=8)


def total8(v):
    v = v[0 : CH // 2] + v[CH // 2 :]
    v = v[0 : CH // 4] + v[CH // 4 :]
    return v[0:8] + v[8:16]


def local_kernel(
    ref, back, place, table, out, high, low,
    gather, xe, ce, states, front, run, kept, pieces, sums, flipped, flat
):
    bt, ct, wr, hr, rates = tables(table)
    make_gather(gather)
    value = jnp.ones((ROWS, LANES), F32)
    for col in reversed(range(COLS)):
        flat[col * ROWS : (col + 1) * ROWS, :] = value * bt[col]
        value = value * wr[col]
    own = own_segment()
    for row in range(ROWS):
        high[row], low[row] = split(diagonal(flat, row, own))
    flip(ref, X0, flipped)
    for two in range(COLS // 2):
        spread(flipped, place, xe, two)
    flip(ref, C0, flipped)
    for two in range(COLS // 2):
        spread(flipped, place, ce, two)
    states[0] = jnp.zeros(BLOCK, F32)
    run[...] = jnp.zeros(BLOCK, F32)

    def forward(col, none):
        total = jnp.zeros((CH, LANES), F32)
        for row in range(ROWS):
            one = slice(row, row + 1)
            state = wr[col, one, :] * states[col, row] + bt[col, one, :] * xe[col, row]
            states[col + 1, row] = state
            total = hr[col, one, :] * total + state
        front[col] = total
        return none

    lax.fori_loop(0, COLS, forward, 0, unroll=UF)
    carry_scan(front, rates, True)

    def products(step, none):
        col = COLS - 1 - step
        carry = back[col]
        for row in reversed(range(ROWS)):
            one = slice(row, row + 1)
            grad = carry + ct[col, one, :] * ce[col, row]
            carry = hr[col, one, :] * grad
            kept[row] = grad
        total = front[col]
        for row in range(ROWS):
            one = slice(row, row + 1)
            grad = kept[row]
            sums[3, row, col] = total8(grad * total)
            total = hr[col, one, :] * total + states[col + 1, row]
            sums[1, row, col] = total8(total * ce[col, row])
            grad = grad + run[row]
            run[row] = wr[col, one, :] * grad
            sums[2, row, col] = total8(grad * states[col, row])
            sums[0, row, col] = total8(grad * xe[col, row])
            high, low = split(grad * bt[col, one, :])
            pieces[col, row * CH : (row + 1) * CH, 0:LANES] = high
            pieces[col, row * CH : (row + 1) * CH, LANES:] = low
        return none

    lax.fori_loop(0, COLS, products, 0, unroll=UP)
    for pair in range(ROWS // 2):
        rows = slice(pair * 2 * CH, (pair + 1) * 2 * CH)
        block = jnp.zeros((2 * CH, 128), F32)
        for col in range(COLS):
            block = block + jnp.dot(pieces[col, rows, :], gather[col], preferred_element_type=F32)
        out[:, pair * COLS : (pair + 1) * COLS, :] = block.T.reshape(SEG, COLS, 2 * CH)
    for which, at in enumerate((I0, O0, W0, W0 + 1)):
        put(ref, out, at, over_sublanes(sums.at[which]))
    out[:, W0 + 2 :, :] = jnp.zeros((SEG, BACK - W0 - 2, 128), F32)


def over_sublanes(part):
    rows = part.reshape(TOKENS * 8, LANES)
    value = rows[pl.ds(0, TOKENS, stride=8), :]
    for k in range(1, 8):
        value = value + rows[pl.ds(k, TOKENS, stride=8), :]
    return value


def put(ref, out, at, value, old=None):
    value = value.T.reshape(SEG, N, TOKENS)
    size = N
    if at >= W0:
        rate = jnp.exp(ref[:, D0 + at - W0 : D0 + at - W0 + 1, :])
        value, size = rate * jnp.sum(value, axis=1, keepdims=True), 1
    if old is not None:
        value = value + old[:, at : at + size, :]
    out[:, at : at + size, :] = value


def outer_kernel(
    ref, edge, local, back, place, table, high, low, out,
    before, after, ce, front, kept, sums, flipped, left, right, flat, raw, meet
):
    bt, ct, wr, hr, rates = tables(table)
    value = jnp.ones((ROWS, LANES), F32)
    for col in range(COLS):
        value = value * wr[col]
        before[col] = value
    value = jnp.ones((ROWS, LANES), F32)
    for col in reversed(range(COLS)):
        after[col] = value
        value = value * wr[col]
    flip(ref, C0, flipped)
    for two in range(COLS // 2):
        spread(flipped, place, ce, two)
    for row in range(ROWS):
        for q in range(QUART):
            part = slice(q * STEP, (q + 1) * STEP)
            left[row, part, :] = edge[row * QUART + q, 0:STEP, :]
            right[row, part, :] = edge[row * QUART + q, STEP : 2 * STEP, :]

    def forward(col, none):
        total = jnp.zeros((CH, LANES), F32)
        for row in range(ROWS):
            one = slice(row, row + 1)
            total = hr[col, one, :] * total + before[col, one, :] * left[row]
        front[col] = total
        return none

    lax.fori_loop(0, COLS, forward, 0)
    carry_scan(front, rates, True)

    def products(col, none):
        carry = back[col]
        for row in reversed(range(ROWS)):
            one = slice(row, row + 1)
            grad = carry + ct[col, one, :] * ce[col, row]
            carry = hr[col, one, :] * grad
            kept[row] = grad
            sums[2, row, col] = total8(grad * left[row])
        total = front[col]
        for row in range(ROWS):
            one = slice(row, row + 1)
            sums[1, row, col] = total8(kept[row] * total)
            total = hr[col, one, :] * total + before[col, one, :] * left[row]
            sums[0, row, col] = total8(total * ce[col, row])
        return none

    lax.fori_loop(0, COLS, products, 0)

    own = own_segment()
    none = jnp.zeros((CH, LANES), BF16)
    half = lax.broadcasted_iota(jnp.int32, (LANES, 128), 1) < CH
    for pair in range(ROWS // 2):
        rows = slice(pair * COLS, (pair + 1) * COLS)
        tokens = ref[:, rows, :].reshape(SEG * COLS, 2 * CH).astype(BF16)
        parts = [split(right[2 * pair + part]) for part in range(2)]
        both = [jnp.concatenate([parts[0][k], parts[1][k]], axis=0) for k in range(2)]
        found = []
        for part in range(2):
            row = 2 * pair + part
            value = jnp.zeros((LANES, LANES), F32)
            for k in range(2):
                pieces = [parts[0][k], none] if part == 0 else [none, parts[1][k]]
                value = value + jnp.dot(tokens, jnp.concatenate(pieces, axis=0), preferred_element_type=F32)
            value = jnp.where(own, value, 0.0).reshape(SEG, COLS, LANES)
            raw[row * COLS : (row + 1) * COLS, :] = jnp.sum(value, axis=0)
            meet[row : row + 1, :] = jnp.sum(right[row] * left[row], axis=0, keepdims=True)
            value = jnp.zeros((LANES, 128), F32)
            for weight, k in ((low, 0), (high, 1), (high, 0)):
                value = value + lax.dot_general(
                    weight[row], both[k], (((1,), (1,)), ((), ())), preferred_element_type=F32
                )
            found.append(value)
        value = jnp.where(half, found[0], found[1]).reshape(SEG, COLS, 128)
        out[:, rows, :] = local[:, rows, :] + value

    put(ref, out, O0, over_sublanes(sums.at[0]), local)
    put(ref, out, W0 + 1, over_sublanes(sums.at[1]), local)
    flat[...] = over_sublanes(sums.at[2])

    def rows_of(a, col):
        return a[pl.ds(col, ROWS, stride=COLS), :]

    value = jnp.zeros((ROWS, LANES), F32)
    terms = [None] * COLS
    for col in reversed(range(COLS)):
        value = rows_of(flat, col) + value
        terms[col] = value * before[col - 1] if col else value
        value = wr[col] * value
    value = meet[...]
    for col in range(COLS):
        terms[col] = terms[col] + after[col] * value
        product = rows_of(raw, col)
        value = wr[col] * value + bt[col] * product
        raw[pl.ds(col, ROWS, stride=COLS), :] = after[col] * product
    for col in range(COLS):
        flat[pl.ds(col, ROWS, stride=COLS), :] = terms[col]
    put(ref, out, I0, raw[...], local)
    put(ref, out, W0, flat[...], local)
    out[:, W0 + 2 :, :] = local[:, W0 + 2 :, :]


WIDE = (COLS, ROWS, CH, LANES)
TOKEN = (COLS, ROWS, LANES)
ENDS = (COLS, CH, LANES)
BLOCK = (ROWS, CH, LANES)
RATES = (COLS, ROWS, LANES)
TABLE = (COLS, 5 * ROWS, LANES)
PLACE = (COLS // 2, LANES, 256)
FLIP = (ROWS * CH, 128)


def vm(shape, kind=F32):
    return pltpu.VMEM(shape, kind)


def call(kernel, ins, outs, scratch, mebibytes, kinds=None, place=pltpu.VMEM, flops=10**8):
    whole = pl.BlockSpec(memory_space=pltpu.VMEM)
    kinds = kinds or (F32,) * len(outs)
    shapes = tuple(jax.ShapeDtypeStruct(s, k) for s, k in zip(outs, kinds))
    single = len(outs) == 1
    return pl.pallas_call(
        kernel,
        out_shape=shapes[0] if single else shapes,
        in_specs=[pl.BlockSpec(memory_space=place)] * ins,
        out_specs=whole if single else (whole,) * len(outs),
        scratch_shapes=scratch,
        compiler_params=pltpu.CompilerParams(vmem_limit_bytes=int(mebibytes * 1024 * 1024)),
        cost_estimate=pl.CostEstimate(flops=flops, bytes_accessed=10**6, transcendentals=0),
    )


def packs():
    scratch = [vm((ROWS, COLS, SEG * CH), BF16)] * 2 + [vm((ROWS, COLS, N))] * 2
    scratch += [vm((ROWS, SEG, COLS))] * 2 + [pltpu.SemaphoreType.DMA((6,))]
    return call(pack_kernel, 6, [(SEG, SENT, 128)], scratch, PK, place=pltpu.HBM)


def edges(devices):
    outs = [(devices, EDGE, LANES), ENDS, TABLE, PLACE]
    scratch = [vm(WIDE), vm((TOKENS, LANES)), vm(RATES), vm(BLOCK), vm(FLIP, BF16)]
    return call(edges_kernel, 1, outs, scratch, 14, kinds=(F32, F32, F32, BF16))


def chains(devices):
    return call(chain_kernel, 1, [(devices, 2 * STEP, LANES)], [], 8)


def local_grads():
    outs = [(SEG, BACK, 128), (ROWS, LANES, LANES), (ROWS, LANES, LANES)]
    scratch = [vm((COLS, 2 * LANES, 128), BF16), vm(WIDE), vm(WIDE), vm((COLS + 1,) + BLOCK), vm(ENDS)]
    scratch += [vm(BLOCK), vm(BLOCK), vm((COLS, ROWS * CH, 2 * LANES), BF16), vm((4, ROWS, COLS, 8, LANES))]
    scratch += [vm(FLIP, BF16), vm((TOKENS, LANES))]
    return call(local_kernel, 4, outs, scratch, 28, kinds=(F32, BF16, BF16), flops=5 * 10**9)


def outer_grads():
    scratch = [vm(TOKEN), vm(TOKEN), vm(WIDE), vm(ENDS), vm(BLOCK), vm((3, ROWS, COLS, 8, LANES))]
    scratch += [vm(FLIP, BF16), vm(BLOCK), vm(BLOCK), vm((TOKENS, LANES)), vm((TOKENS, LANES)), vm((ROWS, LANES))]
    return call(outer_kernel, 8, [(SEG, BACK, 128)], scratch, 16)


def unpacks():
    outs = [(ROWS, COLS, SEG * CH)] + [(ROWS, COLS, N)] * 2 + [(ROWS, SEG, COLS)] * 2
    return call(unpack_kernel, 1, outs, [], 8)


def swapped(a):
    return jnp.transpose(a, (0, 2, 1))


def per_device(tokens, cotangent, state_in, state_out, width_decay, height_decay):
    devices = lax.axis_size("wa")
    message = packs()(
        tokens, cotangent, state_in, state_out, swapped(width_decay), swapped(height_decay)
    )
    tile = lax.all_to_all(message, "ha", 0, 0, tiled=True)
    edge, back, table, place = edges(devices)(tile)
    edge = lax.all_to_all(edge, "wa", 0, 0, tiled=True)
    local, high, low = local_grads()(tile, back, place, table)
    carries = lax.all_to_all(chains(devices)(edge), "wa", 0, 0, tiled=True)
    answer = outer_grads()(tile, carries, local, back, place, table, high, low)
    x, b, s, w, h = unpacks()(lax.all_to_all(answer, "ha", 0, 0, tiled=True))
    return x, b, s, swapped(w), swapped(h)


def solution(mesh):
    spec = P("ha", "wa", None)
    return jax.shard_map(
        per_device, mesh=mesh, in_specs=(spec,) * 6, out_specs=(spec,) * 5, check_vma=False
    )
```

```python
import jax
import jax.numpy as jnp
from jax import lax
from jax.experimental import pallas as pl
from jax.experimental.pallas import tpu as pltpu
from jax.sharding import PartitionSpec as P

F32 = jnp.float32
BF16 = jnp.bfloat16

SEG = 8
ROWS = 8
COLS = 16
CH = 64
N = 16
LANES = SEG * N
TOKENS = ROWS * COLS
STEP = 16
QUART = CH // STEP

X0, C0, B0, S0, D0 = 0, 64, 128, 144, 160
SENT = 162
I0, O0, W0 = 64, 80, 96
BACK = 98
EDGE = 33


def make_place(place):
    k = lax.broadcasted_iota(jnp.int32, (LANES, 256), 0)
    m = lax.broadcasted_iota(jnp.int32, (LANES, 256), 1)
    for two in range(COLS // 2):
        col = 2 * two + m // LANES
        hit = k == ((m % LANES) // N) * COLS + col
        place[two] = jnp.where(hit, 1.0, 0.0).astype(BF16)


def make_gather(gather):
    k = lax.broadcasted_iota(jnp.int32, (2 * LANES, 128), 0)
    m = lax.broadcasted_iota(jnp.int32, (2 * LANES, 128), 1)
    for col in range(COLS):
        hit = m == ((k % LANES) // N) * COLS + col
        gather[col] = jnp.where(hit, 1.0, 0.0).astype(BF16)


def take(ref, at, size, count):
    parts = [ref[g * count + at : g * count + at + size, :][None] for g in range(SEG)]
    return jnp.concatenate(parts, axis=0)


def give(ref, at, count, value):
    for g in range(SEG):
        ref[g * count + at : g * count + at + value.shape[1], :] = value[g]


def pack_kernel(x0, y0, b0, s0, w0, h0, out, x, y, b, s, w, h, done):
    copies = [
        pltpu.make_async_copy(source, target, done.at[k])
        for k, (source, target) in enumerate(((w0, w), (h0, h), (b0, b), (s0, s), (x0, x), (y0, y)))
    ]
    for copy in copies:
        copy.start()
    low = lax.broadcasted_iota(jnp.int32, (COLS, 128), 1) < CH
    for k, (at, a) in enumerate(((D0, w), (D0 + 1, h))):
        copies[k].wait()
        flat = jnp.concatenate([a[row] for row in range(ROWS)], axis=1)
        for g in range(SEG):
            out[g * SENT + at : g * SENT + at + 1, :] = flat[g : g + 1]
    for k, (at, a) in enumerate(((B0, b), (S0, s))):
        copies[2 + k].wait()
        flat = a[...].reshape(TOKENS, N).T
        for g in range(SEG):
            out[g * SENT + at : g * SENT + at + N, :] = flat
    for k, (at, a) in enumerate(((X0, x), (C0, y))):
        copies[4 + k].wait()
        for pair in range(ROWS // 2):
            to = at + pair * COLS
            for two in range(SEG // 2):
                lanes = slice(two * 128, (two + 1) * 128)
                one = a[2 * pair, :, lanes].astype(F32)
                other = a[2 * pair + 1, :, lanes].astype(F32)
                even, odd = 2 * two * SENT + to, (2 * two + 1) * SENT + to
                out[even : even + COLS, :] = jnp.where(low, one, pltpu.roll(other, CH, 1))
                out[odd : odd + COLS, :] = jnp.where(low, pltpu.roll(one, CH, 1), other)


def unpack_kernel(got, x, b, s, w, h):
    low = lax.broadcasted_iota(jnp.int32, (COLS, 128), 1) < CH
    for pair in range(ROWS // 2):
        for two in range(SEG // 2):
            lanes = slice(two * 128, (two + 1) * 128)
            even, odd = 2 * two * BACK + pair * COLS, (2 * two + 1) * BACK + pair * COLS
            one = got[even : even + COLS, :]
            other = got[odd : odd + COLS, :]
            x[2 * pair, :, lanes] = jnp.where(low, one, pltpu.roll(other, CH, 1))
            x[2 * pair + 1, :, lanes] = jnp.where(low, pltpu.roll(one, CH, 1), other)
    for at, a in ((I0, b), (O0, s)):
        flat = got[at : at + N, :]
        for g in range(1, SEG):
            flat = flat + got[g * BACK + at : g * BACK + at + N, :]
        a[...] = flat.T.reshape(ROWS, COLS, N)
    for at, a in ((W0, w), (W0 + 1, h)):
        flat = jnp.concatenate([got[g * BACK + at : g * BACK + at + 1, :] for g in range(SEG)], axis=0)
        for row in range(ROWS):
            a[row] = flat[:, row * COLS : (row + 1) * COLS]


def flip(ref, at, flipped):
    for pair in range(ROWS // 2):
        block = take(ref, at + pair * COLS, COLS, SENT).reshape(SEG * COLS, 2 * CH)
        flipped[pair * 2 * CH : (pair + 1) * 2 * CH, :] = block.T.astype(BF16)


def spread(flipped, place, wide, two):
    for pair in range(ROWS // 2):
        block = flipped[pair * 2 * CH : (pair + 1) * 2 * CH, :]
        out = jnp.dot(block, place[two], preferred_element_type=F32)
        for part in range(2):
            for half in range(2):
                wide[2 * two + half, 2 * pair + part] = out[
                    part * CH : (part + 1) * CH, half * LANES : (half + 1) * LANES
                ]


def by_column(flat, out):
    for col in range(COLS):
        out[col] = flat[pl.ds(col, ROWS, stride=COLS), :]


def small(ref, flat, bt, ct, wr, hr):
    for at, out in ((B0, bt), (S0, ct)):
        flat[...] = take(ref, at, N, SENT).reshape(LANES, TOKENS).T
        by_column(flat, out)
    for at, out in ((D0, wr), (D0 + 1, hr)):
        rate = jnp.exp(take(ref, at, 1, SENT))
        flat[...] = jnp.broadcast_to(rate, (SEG, N, TOKENS)).reshape(LANES, TOKENS).T
        by_column(flat, out)


def tables(rows):
    return [rows.at[:, k * ROWS : (k + 1) * ROWS, :] for k in range(5)]


def mover(down):
    def move(v, by):
        return pltpu.roll(v, by * N if down else LANES - by * N, 1)

    return move


def inside(down):
    lane = lax.broadcasted_iota(jnp.int32, (1, LANES), 1)
    return (lane >= N) if down else (lane < LANES - N)


def carry_rates(flat, rates, down):
    move = mover(down)
    total = flat[0:COLS, :]
    for row in range(1, ROWS):
        total = total * flat[row * COLS : (row + 1) * COLS, :]
    one = jnp.where(inside(down), move(total, 1), 0.0)
    two = one * move(one, 1)
    rates[:, 0, :] = one
    rates[:, 1, :] = two
    rates[:, 2, :] = two * move(two, 2)


def carry_scan(ends, rates, down):
    move = mover(down)
    keep = inside(down)

    def column(col, none):
        f = jnp.where(keep, move(ends[col], 1), 0.0)
        for k, by in enumerate((1, 2, 4)):
            f = f + rates[col, k : k + 1, :] * move(f, by)
        ends[col] = f
        return none

    lax.fori_loop(0, COLS, column, 0, unroll=4)


def split(v):
    high = v.astype(BF16)
    return high, (v - high.astype(F32)).astype(BF16)


def own_segment():
    r = lax.broadcasted_iota(jnp.int32, (LANES, LANES), 0)
    m = lax.broadcasted_iota(jnp.int32, (LANES, LANES), 1)
    return r // COLS == m // N


def diagonal(flat, row, own):
    value = flat[pl.ds(row, COLS, stride=ROWS), :]
    return jnp.where(own, jnp.concatenate([value] * SEG, axis=0), 0.0)


def edges_kernel(ref, edge, back, rows, place, ce, flat, rates, head, flipped):
    make_place(place)
    bt, ct, wr, hr, down = tables(rows)
    small(ref, flat, bt, ct, wr, hr)
    carry_rates(flat, rates, False)
    carry_rates(flat, down, True)
    flip(ref, C0, flipped)
    for two in range(COLS // 2):
        spread(flipped, place, ce, two)

    def ends(col, none):
        carry = jnp.zeros((CH, LANES), F32)
        for row in reversed(range(ROWS)):
            one = slice(row, row + 1)
            carry = hr[col, one, :] * (carry + ct[col, one, :] * ce[col, row])
        back[col] = carry
        return none

    lax.fori_loop(0, COLS, ends, 0, unroll=2)
    carry_scan(back, rates, False)

    after = jnp.ones((ROWS, LANES), F32)
    for col in reversed(range(COLS)):
        flat[col * ROWS : (col + 1) * ROWS, :] = after * bt[col]
        after = after * wr[col]
    own = own_segment()
    flip(ref, X0, flipped)
    for pair in range(ROWS // 2):
        for part in range(2):
            row = 2 * pair + part
            high, low = split(diagonal(flat, row, own))
            mine = flipped[row * CH : (row + 1) * CH, :]
            tail = jnp.dot(mine, high, preferred_element_type=F32) + jnp.dot(
                mine, low, preferred_element_type=F32
            )
            for q in range(QUART):
                at = (row * QUART + q) * EDGE
                edge[at : at + STEP, :] = tail[q * STEP : (q + 1) * STEP]
                edge[at + 2 * STEP : at + EDGE, :] = after[row : row + 1]

    head[...] = jnp.zeros_like(head)

    def sums(step, none):
        col = COLS - 1 - 2 * step
        carry, carry2 = back[col], back[col - 1]
        for row in reversed(range(ROWS)):
            one = slice(row, row + 1)
            grad = carry + ct[col, one, :] * ce[col, row]
            carry = hr[col, one, :] * grad
            grad2 = carry2 + ct[col - 1, one, :] * ce[col - 1, row]
            carry2 = hr[col - 1, one, :] * grad2
            head[row] = wr[col - 1, one, :] * (wr[col, one, :] * (head[row] + grad) + grad2)
        return none

    lax.fori_loop(0, COLS // 2, sums, 0)
    for row in range(ROWS):
        for q in range(QUART):
            at = (row * QUART + q) * EDGE + STEP
            edge[at : at + STEP, :] = head[row, q * STEP : (q + 1) * STEP, :]


def chain_kernel(got, out):
    count = out.shape[0]
    right = left = jnp.zeros((STEP, LANES), F32)
    for hop in range(count):
        place = count - 1 - hop
        out[hop, 0:STEP, :] = right
        out[place, STEP : 2 * STEP, :] = left
        one, other = hop * EDGE, place * EDGE
        right = got[one + 2 * STEP : one + EDGE, :] * right + got[one : one + STEP, :]
        left = got[other + 2 * STEP : other + EDGE, :] * left + got[other + STEP : other + 2 * STEP, :]


def total8(v):
    v = v[0 : CH // 2] + v[CH // 2 :]
    v = v[0 : CH // 4] + v[CH // 4 :]
    return v[0:8] + v[8:16]


def local_kernel(
    ref, back, place, table, out, high, low, far_ce, far_grad,
    gather, xe, ce, states, front, run, kept, pieces, sums, flipped, flat, done
):
    bt, ct, wr, hr, rates = tables(table)
    make_gather(gather)
    value = jnp.ones((ROWS, LANES), F32)
    for col in reversed(range(COLS)):
        flat[col * ROWS : (col + 1) * ROWS, :] = value * bt[col]
        value = value * wr[col]
    own = own_segment()
    for row in range(ROWS):
        high[row], low[row] = split(diagonal(flat, row, own))
    flip(ref, X0, flipped)
    for two in range(COLS // 2):
        spread(flipped, place, xe, two)
    flip(ref, C0, flipped)
    for two in range(COLS // 2):
        spread(flipped, place, ce, two)
    copies = [
        pltpu.make_async_copy(source, target, done.at[k])
        for k, (source, target) in enumerate(((ce, far_ce), (kept, far_grad)))
    ]
    copies[0].start()
    states[0] = jnp.zeros(BLOCK, F32)
    run[...] = jnp.zeros(BLOCK, F32)

    def forward(col, none):
        total = jnp.zeros((CH, LANES), F32)
        for row in range(ROWS):
            one = slice(row, row + 1)
            state = wr[col, one, :] * states[col, row] + bt[col, one, :] * xe[col, row]
            states[col + 1, row] = state
            total = hr[col, one, :] * total + state
        front[col] = total
        return none

    lax.fori_loop(0, COLS, forward, 0)
    carry_scan(front, rates, True)

    def products(step, none):
        col = COLS - 1 - step
        carry = back[col]
        for row in reversed(range(ROWS)):
            one = slice(row, row + 1)
            grad = carry + ct[col, one, :] * ce[col, row]
            carry = hr[col, one, :] * grad
            kept[col, row] = grad
        total = front[col]
        for row in range(ROWS):
            one = slice(row, row + 1)
            grad = kept[col, row]
            sums[3, row, col] = total8(grad * total)
            total = hr[col, one, :] * total + states[col + 1, row]
            sums[1, row, col] = total8(total * ce[col, row])
            grad = grad + run[row]
            run[row] = wr[col, one, :] * grad
            sums[2, row, col] = total8(grad * states[col, row])
            sums[0, row, col] = total8(grad * xe[col, row])
            high, low = split(grad * bt[col, one, :])
            pieces[col, row * CH : (row + 1) * CH, 0:LANES] = high
            pieces[col, row * CH : (row + 1) * CH, LANES:] = low
        return none

    lax.fori_loop(0, COLS, products, 0)
    copies[1].start()
    for pair in range(ROWS // 2):
        rows = slice(pair * 2 * CH, (pair + 1) * 2 * CH)
        block = jnp.zeros((2 * CH, 128), F32)
        for col in range(COLS):
            block = block + jnp.dot(pieces[col, rows, :], gather[col], preferred_element_type=F32)
        give(out, pair * COLS, BACK, block.T.reshape(SEG, COLS, 2 * CH))
    for which, at in enumerate((I0, O0, W0, W0 + 1)):
        put(ref, out, at, over_sublanes(sums.at[which]))
    for copy in copies:
        copy.wait()


def over_sublanes(part):
    rows = part.reshape(TOKENS * 8, LANES)
    value = rows[pl.ds(0, TOKENS, stride=8), :]
    for k in range(1, 8):
        value = value + rows[pl.ds(k, TOKENS, stride=8), :]
    return value


def put(ref, out, at, value, old=None):
    value = value.T.reshape(SEG, N, TOKENS)
    size = N
    if at >= W0:
        rate = jnp.exp(take(ref, D0 + at - W0, 1, SENT))
        value, size = rate * jnp.sum(value, axis=1, keepdims=True), 1
    if old is not None:
        value = value + take(old, at, size, BACK)
    give(out, at, BACK, value)


def outer_kernel(
    ref, edge, local, table, high, low, far_ce, far_grad, out,
    before, after, ce, inner, front, sums, left, right, flat, raw, meet, done
):
    def fetch(col):
        return (
            pltpu.make_async_copy(far_grad.at[col], inner.at[col], done.at[0, col]),
            pltpu.make_async_copy(far_ce.at[col], ce.at[col], done.at[1, col]),
        )

    for col in range(COLS):
        for copy in fetch(col):
            copy.start()
    bt, ct, wr, hr, rates = tables(table)
    value = jnp.ones((ROWS, LANES), F32)
    for col in range(COLS):
        value = value * wr[col]
        before[col] = value
    value = jnp.ones((ROWS, LANES), F32)
    for col in reversed(range(COLS)):
        after[col] = value
        value = value * wr[col]
    for row in range(ROWS):
        for q in range(QUART):
            part = slice(q * STEP, (q + 1) * STEP)
            left[row, part, :] = edge[row * QUART + q, 0:STEP, :]
            right[row, part, :] = edge[row * QUART + q, STEP : 2 * STEP, :]

    def forward(col, none):
        total = jnp.zeros((CH, LANES), F32)
        for row in range(ROWS):
            one = slice(row, row + 1)
            total = hr[col, one, :] * total + before[col, one, :] * left[row]
        front[col] = total
        return none

    lax.fori_loop(0, COLS, forward, 0)
    carry_scan(front, rates, True)

    def products(col, none):
        for copy in fetch(col):
            copy.wait()
        total = front[col]
        for row in range(ROWS):
            one = slice(row, row + 1)
            grad = inner[col, row]
            sums[2, row, col] = total8(grad * left[row])
            sums[1, row, col] = total8(grad * total)
            total = hr[col, one, :] * total + before[col, one, :] * left[row]
            sums[0, row, col] = total8(total * ce[col, row])
        return none

    lax.fori_loop(0, COLS, products, 0)

    own = own_segment()
    none = jnp.zeros((CH, LANES), BF16)
    half = lax.broadcasted_iota(jnp.int32, (LANES, 128), 1) < CH
    for pair in range(ROWS // 2):
        tokens = take(ref, X0 + pair * COLS, COLS, SENT).reshape(SEG * COLS, 2 * CH).astype(BF16)
        parts = [split(right[2 * pair + part]) for part in range(2)]
        both = [jnp.concatenate([parts[0][k], parts[1][k]], axis=0) for k in range(2)]
        found = []
        for part in range(2):
            row = 2 * pair + part
            value = jnp.zeros((LANES, LANES), F32)
            for k in range(2):
                pieces = [parts[0][k], none] if part == 0 else [none, parts[1][k]]
                value = value + jnp.dot(tokens, jnp.concatenate(pieces, axis=0), preferred_element_type=F32)
            value = jnp.where(own, value, 0.0).reshape(SEG, COLS, LANES)
            raw[row * COLS : (row + 1) * COLS, :] = jnp.sum(value, axis=0)
            meet[row : row + 1, :] = jnp.sum(right[row] * left[row], axis=0, keepdims=True)
            value = jnp.zeros((LANES, 128), F32)
            for weight, k in ((low, 0), (high, 1), (high, 0)):
                value = value + lax.dot_general(
                    weight[row], both[k], (((1,), (1,)), ((), ())), preferred_element_type=F32
                )
            found.append(value)
        value = jnp.where(half, found[0], found[1]).reshape(SEG, COLS, 128)
        give(out, pair * COLS, BACK, take(local, pair * COLS, COLS, BACK) + value)

    put(ref, out, O0, over_sublanes(sums.at[0]), local)
    put(ref, out, W0 + 1, over_sublanes(sums.at[1]), local)
    flat[...] = over_sublanes(sums.at[2])

    def rows_of(a, col):
        return a[pl.ds(col, ROWS, stride=COLS), :]

    value = jnp.zeros((ROWS, LANES), F32)
    terms = [None] * COLS
    for col in reversed(range(COLS)):
        value = rows_of(flat, col) + value
        terms[col] = value * before[col - 1] if col else value
        value = wr[col] * value
    value = meet[...]
    for col in range(COLS):
        terms[col] = terms[col] + after[col] * value
        product = rows_of(raw, col)
        value = wr[col] * value + bt[col] * product
        raw[pl.ds(col, ROWS, stride=COLS), :] = after[col] * product
    for col in range(COLS):
        flat[pl.ds(col, ROWS, stride=COLS), :] = terms[col]
    put(ref, out, I0, raw[...], local)
    put(ref, out, W0, flat[...], local)


WIDE = (COLS, ROWS, CH, LANES)
TOKEN = (COLS, ROWS, LANES)
ENDS = (COLS, CH, LANES)
BLOCK = (ROWS, CH, LANES)
RATES = (COLS, ROWS, LANES)
TABLE = (COLS, 5 * ROWS, LANES)
PLACE = (COLS // 2, LANES, 256)
FLIP = (ROWS * CH, 128)


def vm(shape, kind=F32):
    return pltpu.VMEM(shape, kind)


def call(kernel, ins, outs, scratch, mebibytes, kinds=None, place=pltpu.VMEM, flops=10**8, far_in=0, far_out=0):
    near, far = pl.BlockSpec(memory_space=place), pl.BlockSpec(memory_space=pltpu.HBM)
    whole = pl.BlockSpec(memory_space=pltpu.VMEM)
    kinds = kinds or (F32,) * len(outs)
    shapes = tuple(jax.ShapeDtypeStruct(s, k) for s, k in zip(outs, kinds))
    single = len(outs) == 1
    return pl.pallas_call(
        kernel,
        out_shape=shapes[0] if single else shapes,
        in_specs=[near] * (ins - far_in) + [far] * far_in,
        out_specs=whole if single else (whole,) * (len(outs) - far_out) + (far,) * far_out,
        scratch_shapes=scratch,
        compiler_params=pltpu.CompilerParams(vmem_limit_bytes=int(mebibytes * 1024 * 1024)),
        cost_estimate=pl.CostEstimate(flops=flops, bytes_accessed=10**6, transcendentals=0),
    )


def packs():
    scratch = [vm((ROWS, COLS, SEG * CH), BF16)] * 2 + [vm((ROWS, COLS, N))] * 2
    scratch += [vm((ROWS, SEG, COLS))] * 2 + [pltpu.SemaphoreType.DMA((6,))]
    return call(pack_kernel, 6, [(SEG * SENT, 128)], scratch, 60, place=pltpu.HBM)


def edges(devices):
    outs = [(devices * EDGE, LANES), ENDS, TABLE, PLACE]
    scratch = [vm(WIDE), vm((TOKENS, LANES)), vm(RATES), vm(BLOCK), vm(FLIP, BF16)]
    return call(edges_kernel, 1, outs, scratch, 14, kinds=(F32, F32, F32, BF16))


def chains(devices):
    return call(chain_kernel, 1, [(devices, 2 * STEP, LANES)], [], 8)


def local_grads():
    outs = [(SEG * BACK, 128), (ROWS, LANES, LANES), (ROWS, LANES, LANES), WIDE, WIDE]
    scratch = [vm((COLS, 2 * LANES, 128), BF16), vm(WIDE), vm(WIDE), vm((COLS + 1,) + BLOCK), vm(ENDS)]
    scratch += [vm(BLOCK), vm(WIDE), vm((COLS, ROWS * CH, 2 * LANES), BF16), vm((4, ROWS, COLS, 8, LANES))]
    scratch += [vm(FLIP, BF16), vm((TOKENS, LANES)), pltpu.SemaphoreType.DMA((2,))]
    kinds = (F32, BF16, BF16, F32, F32)
    return call(local_kernel, 4, outs, scratch, 50, kinds=kinds, flops=5 * 10**9, far_out=2)


def outer_grads():
    scratch = [vm(TOKEN), vm(TOKEN), vm(WIDE), vm(WIDE), vm(ENDS), vm((3, ROWS, COLS, 8, LANES)), vm(BLOCK)]
    scratch += [vm(BLOCK), vm((TOKENS, LANES)), vm((TOKENS, LANES)), vm((ROWS, LANES))]
    scratch += [pltpu.SemaphoreType.DMA((2, COLS))]
    return call(outer_kernel, 8, [(SEG * BACK, 128)], scratch, 50, far_in=2)


def unpacks():
    outs = [(ROWS, COLS, SEG * CH)] + [(ROWS, COLS, N)] * 2 + [(ROWS, SEG, COLS)] * 2
    return call(unpack_kernel, 1, outs, [], 8)


def exchange(a, axis):
    return lax.all_to_all(a.reshape(-1, 1, LANES), axis, 0, 0, tiled=True).reshape(-1, LANES)


def swapped(a):
    return jnp.transpose(a, (0, 2, 1))


def per_device(tokens, cotangent, state_in, state_out, width_decay, height_decay):
    devices = lax.axis_size("wa")
    message = packs()(
        tokens, cotangent, state_in, state_out, swapped(width_decay), swapped(height_decay)
    )
    tile = exchange(message, "ha")
    edge, back, table, place = edges(devices)(tile)
    edge = exchange(edge, "wa")
    local, high, low, *far = local_grads()(tile, back, place, table)
    carries = lax.all_to_all(chains(devices)(edge), "wa", 0, 0, tiled=True)
    answer = outer_grads()(tile, carries, local, table, high, low, *far)
    x, b, s, w, h = unpacks()(exchange(answer, "ha"))
    return x, b, s, swapped(w), swapped(h)


def solution(mesh):
    spec = P("ha", "wa", None)
    return jax.shard_map(
        per_device, mesh=mesh, in_specs=(spec,) * 6, out_specs=(spec,) * 5, check_vma=False
    )
```

```python
import jax
import jax.numpy as jnp
from jax import lax
from jax.experimental import pallas as pl
from jax.experimental.pallas import tpu as pltpu
from jax.sharding import PartitionSpec as P

F32 = jnp.float32
BF16 = jnp.bfloat16

SEG = 8
ROWS = 8
COLS = 16
CH = 64
N = 16
LANES = SEG * N
TOKENS = ROWS * COLS
STEP = 16
QUART = CH // STEP

X0, C0, B0, S0, D0 = 0, 64, 128, 144, 160
SENT = 162
I0, O0, W0 = 64, 80, 96
BACK = 98
EDGE = 33


def make_place(place):
    k = lax.broadcasted_iota(jnp.int32, (LANES, 256), 0)
    m = lax.broadcasted_iota(jnp.int32, (LANES, 256), 1)
    for two in range(COLS // 2):
        col = 2 * two + m // LANES
        hit = k == ((m % LANES) // N) * COLS + col
        place[two] = jnp.where(hit, 1.0, 0.0).astype(BF16)


def make_gather(gather):
    k = lax.broadcasted_iota(jnp.int32, (2 * LANES, 128), 0)
    m = lax.broadcasted_iota(jnp.int32, (2 * LANES, 128), 1)
    for col in range(COLS):
        hit = m == ((k % LANES) // N) * COLS + col
        gather[col] = jnp.where(hit, 1.0, 0.0).astype(BF16)


def take(ref, at, size, count):
    parts = [ref[g * count + at : g * count + at + size, :][None] for g in range(SEG)]
    return jnp.concatenate(parts, axis=0)


def give(ref, at, count, value):
    for g in range(SEG):
        ref[g * count + at : g * count + at + value.shape[1], :] = value[g]


def pack_kernel(x0, y0, b0, s0, w0, h0, out, x, y, b, s, w, h, done):
    copies = [
        pltpu.make_async_copy(source, target, done.at[k])
        for k, (source, target) in enumerate(((w0, w), (h0, h), (b0, b), (s0, s), (x0, x), (y0, y)))
    ]
    for copy in copies:
        copy.start()
    low = lax.broadcasted_iota(jnp.int32, (COLS, 128), 1) < CH
    for k, (at, a) in enumerate(((D0, w), (D0 + 1, h))):
        copies[k].wait()
        flat = jnp.concatenate([a[row] for row in range(ROWS)], axis=1)
        for g in range(SEG):
            out[g * SENT + at : g * SENT + at + 1, :] = flat[g : g + 1]
    for k, (at, a) in enumerate(((B0, b), (S0, s))):
        copies[2 + k].wait()
        flat = a[...].reshape(TOKENS, N).T
        for g in range(SEG):
            out[g * SENT + at : g * SENT + at + N, :] = flat
    for k, (at, a) in enumerate(((X0, x), (C0, y))):
        copies[4 + k].wait()
        for pair in range(ROWS // 2):
            to = at + pair * COLS
            for two in range(SEG // 2):
                lanes = slice(two * 128, (two + 1) * 128)
                one = a[2 * pair, :, lanes].astype(F32)
                other = a[2 * pair + 1, :, lanes].astype(F32)
                even, odd = 2 * two * SENT + to, (2 * two + 1) * SENT + to
                out[even : even + COLS, :] = jnp.where(low, one, pltpu.roll(other, CH, 1))
                out[odd : odd + COLS, :] = jnp.where(low, pltpu.roll(one, CH, 1), other)


def unpack_kernel(got, x, b, s, w, h):
    low = lax.broadcasted_iota(jnp.int32, (COLS, 128), 1) < CH
    for pair in range(ROWS // 2):
        for two in range(SEG // 2):
            lanes = slice(two * 128, (two + 1) * 128)
            even, odd = 2 * two * BACK + pair * COLS, (2 * two + 1) * BACK + pair * COLS
            one = got[even : even + COLS, :]
            other = got[odd : odd + COLS, :]
            x[2 * pair, :, lanes] = jnp.where(low, one, pltpu.roll(other, CH, 1))
            x[2 * pair + 1, :, lanes] = jnp.where(low, pltpu.roll(one, CH, 1), other)
    for at, a in ((I0, b), (O0, s)):
        flat = got[at : at + N, :]
        for g in range(1, SEG):
            flat = flat + got[g * BACK + at : g * BACK + at + N, :]
        a[...] = flat.T.reshape(ROWS, COLS, N)
    for at, a in ((W0, w), (W0 + 1, h)):
        flat = jnp.concatenate([got[g * BACK + at : g * BACK + at + 1, :] for g in range(SEG)], axis=0)
        for row in range(ROWS):
            a[row] = flat[:, row * COLS : (row + 1) * COLS]


def flip(ref, at, flipped):
    for pair in range(ROWS // 2):
        block = take(ref, at + pair * COLS, COLS, SENT).reshape(SEG * COLS, 2 * CH)
        flipped[pair * 2 * CH : (pair + 1) * 2 * CH, :] = block.T.astype(BF16)


def spread(flipped, place, wide, two, thin=None):
    for pair in range(ROWS // 2):
        block = flipped[pair * 2 * CH : (pair + 1) * 2 * CH, :]
        out = jnp.dot(block, place[two], preferred_element_type=F32)
        for part in range(2):
            for half in range(2):
                value = out[part * CH : (part + 1) * CH, half * LANES : (half + 1) * LANES]
                wide[2 * two + half, 2 * pair + part] = value
                if thin is not None:
                    thin[2 * two + half, 2 * pair + part] = value.astype(BF16)


def by_column(flat, out):
    for col in range(COLS):
        out[col] = flat[pl.ds(col, ROWS, stride=COLS), :]


def small(ref, flat, bt, ct, wr, hr):
    for at, out in ((B0, bt), (S0, ct)):
        flat[...] = take(ref, at, N, SENT).reshape(LANES, TOKENS).T
        by_column(flat, out)
    for at, out in ((D0, wr), (D0 + 1, hr)):
        rate = jnp.exp(take(ref, at, 1, SENT))
        flat[...] = jnp.broadcast_to(rate, (SEG, N, TOKENS)).reshape(LANES, TOKENS).T
        by_column(flat, out)


def tables(rows):
    return [rows.at[:, k * ROWS : (k + 1) * ROWS, :] for k in range(5)]


def mover(down):
    def move(v, by):
        return pltpu.roll(v, by * N if down else LANES - by * N, 1)

    return move


def inside(down):
    lane = lax.broadcasted_iota(jnp.int32, (1, LANES), 1)
    return (lane >= N) if down else (lane < LANES - N)


def carry_rates(flat, rates, down):
    move = mover(down)
    total = flat[0:COLS, :]
    for row in range(1, ROWS):
        total = total * flat[row * COLS : (row + 1) * COLS, :]
    one = jnp.where(inside(down), move(total, 1), 0.0)
    two = one * move(one, 1)
    rates[:, 0, :] = one
    rates[:, 1, :] = two
    rates[:, 2, :] = two * move(two, 2)


def carry_scan(ends, rates, down):
    move = mover(down)
    keep = inside(down)

    for part in range(2):
        cols = range(part * COLS // 2, (part + 1) * COLS // 2)
        values = [jnp.where(keep, move(ends[col], 1), 0.0) for col in cols]
        for k, by in enumerate((1, 2, 4)):
            moved = [move(f, by) for f in values]
            values = [f + rates[col, k : k + 1, :] * g for col, f, g in zip(cols, values, moved)]
        for col, f in zip(cols, values):
            ends[col] = f


def split(v):
    high = v.astype(BF16)
    return high, (v - high.astype(F32)).astype(BF16)


def own_segment():
    r = lax.broadcasted_iota(jnp.int32, (LANES, LANES), 0)
    m = lax.broadcasted_iota(jnp.int32, (LANES, LANES), 1)
    return r // COLS == m // N


def diagonal(flat, row, own):
    value = flat[pl.ds(row, COLS, stride=ROWS), :]
    return jnp.where(own, jnp.concatenate([value] * SEG, axis=0), 0.0)


def edges_kernel(ref, edge, back, rows, place, ce, flat, rates, head, flipped):
    make_place(place)
    bt, ct, wr, hr, down = tables(rows)
    small(ref, flat, bt, ct, wr, hr)
    carry_rates(flat, rates, False)
    carry_rates(flat, down, True)
    flip(ref, C0, flipped)
    for two in range(COLS // 2):
        spread(flipped, place, ce, two)

    def ends(step, none):
        cols = [step * 4 + k for k in range(4)]
        carries = [jnp.zeros((CH, LANES), F32)] * 4
        for row in reversed(range(ROWS)):
            one = slice(row, row + 1)
            carries = [hr[c, one, :] * (v + ct[c, one, :] * ce[c, row]) for c, v in zip(cols, carries)]
        for c, v in zip(cols, carries):
            back[c] = v
        return none

    lax.fori_loop(0, COLS // 4, ends, 0)
    carry_scan(back, rates, False)

    after = jnp.ones((ROWS, LANES), F32)
    for col in reversed(range(COLS)):
        flat[col * ROWS : (col + 1) * ROWS, :] = after * bt[col]
        after = after * wr[col]
    own = own_segment()
    flip(ref, X0, flipped)
    for pair in range(ROWS // 2):
        for part in range(2):
            row = 2 * pair + part
            high, low = split(diagonal(flat, row, own))
            mine = flipped[row * CH : (row + 1) * CH, :]
            tail = jnp.dot(mine, high, preferred_element_type=F32) + jnp.dot(
                mine, low, preferred_element_type=F32
            )
            for q in range(QUART):
                at = (row * QUART + q) * EDGE
                edge[at : at + STEP, :] = tail[q * STEP : (q + 1) * STEP]
                edge[at + 2 * STEP : at + EDGE, :] = after[row : row + 1]

    head[...] = jnp.zeros_like(head)

    def sums(step, none):
        col = COLS - 1 - 2 * step
        carry, carry2 = back[col], back[col - 1]
        for row in reversed(range(ROWS)):
            one = slice(row, row + 1)
            grad = carry + ct[col, one, :] * ce[col, row]
            carry = hr[col, one, :] * grad
            grad2 = carry2 + ct[col - 1, one, :] * ce[col - 1, row]
            carry2 = hr[col - 1, one, :] * grad2
            head[row] = wr[col - 1, one, :] * (wr[col, one, :] * (head[row] + grad) + grad2)
        return none

    lax.fori_loop(0, COLS // 2, sums, 0)
    for row in range(ROWS):
        for q in range(QUART):
            at = (row * QUART + q) * EDGE + STEP
            edge[at : at + STEP, :] = head[row, q * STEP : (q + 1) * STEP, :]


def chain_kernel(got, out):
    count = out.shape[0]
    right = left = jnp.zeros((STEP, LANES), F32)
    for hop in range(count):
        place = count - 1 - hop
        out[hop, 0:STEP, :] = right
        out[place, STEP : 2 * STEP, :] = left
        one, other = hop * EDGE, place * EDGE
        right = got[one + 2 * STEP : one + EDGE, :] * right + got[one : one + STEP, :]
        left = got[other + 2 * STEP : other + EDGE, :] * left + got[other + STEP : other + 2 * STEP, :]


def total8(v):
    v = v[0 : CH // 2] + v[CH // 2 :]
    v = v[0 : CH // 4] + v[CH // 4 :]
    return v[0:8] + v[8:16]


def local_kernel(
    ref, back, place, table, out, high, low, far_ce, far_grad,
    gather, xe, ce, states, front, run, kept, pieces, sums, flipped, flat, thin, done
):
    bt, ct, wr, hr, rates = tables(table)
    make_gather(gather)
    value = jnp.ones((ROWS, LANES), F32)
    for col in reversed(range(COLS)):
        flat[col * ROWS : (col + 1) * ROWS, :] = value * bt[col]
        value = value * wr[col]
    own = own_segment()
    for row in range(ROWS):
        high[row], low[row] = split(diagonal(flat, row, own))
    flip(ref, X0, flipped)
    for two in range(COLS // 2):
        spread(flipped, place, xe, two)
    flip(ref, C0, flipped)
    for two in range(COLS // 2):
        spread(flipped, place, ce, two, thin)
    copies = [
        pltpu.make_async_copy(source, target, done.at[k])
        for k, (source, target) in enumerate(((thin, far_ce), (kept, far_grad)))
    ]
    copies[0].start()
    states[0] = jnp.zeros(BLOCK, F32)
    run[...] = jnp.zeros(BLOCK, F32)

    def forward(col, none):
        total = jnp.zeros((CH, LANES), F32)
        for row in range(ROWS):
            one = slice(row, row + 1)
            state = wr[col, one, :] * states[col, row] + bt[col, one, :] * xe[col, row]
            states[col + 1, row] = state
            total = hr[col, one, :] * total + state
        front[col] = total
        return none

    lax.fori_loop(0, COLS, forward, 0)
    carry_scan(front, rates, True)

    def products(step, none):
        col = COLS - 1 - step
        carry = back[col]
        for row in reversed(range(ROWS)):
            one = slice(row, row + 1)
            grad = carry + ct[col, one, :] * ce[col, row]
            carry = hr[col, one, :] * grad
            kept[col, row] = grad
        total = front[col]
        for row in range(ROWS):
            one = slice(row, row + 1)
            grad = kept[col, row]
            sums[3, row, col] = total8(grad * total)
            total = hr[col, one, :] * total + states[col + 1, row]
            sums[1, row, col] = total8(total * ce[col, row])
            grad = grad + run[row]
            run[row] = wr[col, one, :] * grad
            sums[2, row, col] = total8(grad * states[col, row])
            sums[0, row, col] = total8(grad * xe[col, row])
            high, low = split(grad * bt[col, one, :])
            pieces[col, row * CH : (row + 1) * CH, 0:LANES] = high
            pieces[col, row * CH : (row + 1) * CH, LANES:] = low
        return none

    lax.fori_loop(0, COLS, products, 0)
    copies[1].start()
    for pair in range(ROWS // 2):
        rows = slice(pair * 2 * CH, (pair + 1) * 2 * CH)
        block = jnp.zeros((2 * CH, 128), F32)
        for col in range(COLS):
            block = block + jnp.dot(pieces[col, rows, :], gather[col], preferred_element_type=F32)
        give(out, pair * COLS, BACK, block.T.reshape(SEG, COLS, 2 * CH))
    for which, at in enumerate((I0, O0, W0, W0 + 1)):
        put(ref, out, at, over_sublanes(sums.at[which]))
    for copy in copies:
        copy.wait()


def over_sublanes(part):
    rows = part.reshape(TOKENS * 8, LANES)
    value = rows[pl.ds(0, TOKENS, stride=8), :]
    for k in range(1, 8):
        value = value + rows[pl.ds(k, TOKENS, stride=8), :]
    return value


def put(ref, out, at, value, old=None):
    value = value.T.reshape(SEG, N, TOKENS)
    size = N
    if at >= W0:
        rate = jnp.exp(take(ref, D0 + at - W0, 1, SENT))
        value, size = rate * jnp.sum(value, axis=1, keepdims=True), 1
    if old is not None:
        value = value + take(old, at, size, BACK)
    give(out, at, BACK, value)


def outer_kernel(
    ref, edge, local, table, high, low, far_ce, far_grad, out,
    before, after, ce, inner, front, sums, left, right, flat, raw, meet, done
):
    def fetch(col):
        return (
            pltpu.make_async_copy(far_grad.at[col], inner.at[col], done.at[0, col]),
            pltpu.make_async_copy(far_ce.at[col], ce.at[col], done.at[1, col]),
        )

    for col in range(COLS):
        for copy in fetch(col):
            copy.start()
    bt, ct, wr, hr, rates = tables(table)
    value = jnp.ones((ROWS, LANES), F32)
    for col in range(COLS):
        value = value * wr[col]
        before[col] = value
    value = jnp.ones((ROWS, LANES), F32)
    for col in reversed(range(COLS)):
        after[col] = value
        value = value * wr[col]
    for row in range(ROWS):
        for q in range(QUART):
            part = slice(q * STEP, (q + 1) * STEP)
            left[row, part, :] = edge[row * QUART + q, 0:STEP, :]
            right[row, part, :] = edge[row * QUART + q, STEP : 2 * STEP, :]

    own = own_segment()
    empty = jnp.zeros((CH, LANES), BF16)
    half = lax.broadcasted_iota(jnp.int32, (LANES, 128), 1) < CH
    for pair in range(ROWS // 2):
        tokens = take(ref, X0 + pair * COLS, COLS, SENT).reshape(SEG * COLS, 2 * CH).astype(BF16)
        parts = [split(right[2 * pair + part]) for part in range(2)]
        both = [jnp.concatenate([parts[0][k], parts[1][k]], axis=0) for k in range(2)]
        found = []
        for part in range(2):
            row = 2 * pair + part
            value = jnp.zeros((LANES, LANES), F32)
            for k in range(2):
                pieces = [parts[0][k], empty] if part == 0 else [empty, parts[1][k]]
                value = value + jnp.dot(tokens, jnp.concatenate(pieces, axis=0), preferred_element_type=F32)
            value = jnp.where(own, value, 0.0).reshape(SEG, COLS, LANES)
            raw[row * COLS : (row + 1) * COLS, :] = jnp.sum(value, axis=0)
            meet[row : row + 1, :] = jnp.sum(right[row] * left[row], axis=0, keepdims=True)
            value = jnp.zeros((LANES, 128), F32)
            for weight, k in ((low, 0), (high, 1), (high, 0)):
                value = value + lax.dot_general(
                    weight[row], both[k], (((1,), (1,)), ((), ())), preferred_element_type=F32
                )
            found.append(value)
        value = jnp.where(half, found[0], found[1]).reshape(SEG, COLS, 128)
        give(out, pair * COLS, BACK, take(local, pair * COLS, COLS, BACK) + value)

    def forward(step, none):
        cols = [step * 4 + k for k in range(4)]
        totals = [jnp.zeros((CH, LANES), F32)] * 4
        for row in range(ROWS):
            one = slice(row, row + 1)
            enter = left[row]
            totals = [hr[c, one, :] * v + before[c, one, :] * enter for c, v in zip(cols, totals)]
        for c, v in zip(cols, totals):
            front[c] = v
        return none

    lax.fori_loop(0, COLS // 4, forward, 0)
    carry_scan(front, rates, True)

    def products(col, none):
        for copy in fetch(col):
            copy.wait()
        total = front[col]
        for row in range(ROWS):
            one = slice(row, row + 1)
            grad = inner[col, row]
            sums[2, row, col] = total8(grad * left[row])
            sums[1, row, col] = total8(grad * total)
            total = hr[col, one, :] * total + before[col, one, :] * left[row]
            sums[0, row, col] = total8(total * ce[col, row].astype(F32))
        return none

    lax.fori_loop(0, COLS, products, 0)

    put(ref, out, O0, over_sublanes(sums.at[0]), local)
    put(ref, out, W0 + 1, over_sublanes(sums.at[1]), local)
    flat[...] = over_sublanes(sums.at[2])

    def rows_of(a, col):
        return a[pl.ds(col, ROWS, stride=COLS), :]

    value = jnp.zeros((ROWS, LANES), F32)
    terms = [None] * COLS
    for col in reversed(range(COLS)):
        value = rows_of(flat, col) + value
        terms[col] = value * before[col - 1] if col else value
        value = wr[col] * value
    value = meet[...]
    for col in range(COLS):
        terms[col] = terms[col] + after[col] * value
        product = rows_of(raw, col)
        value = wr[col] * value + bt[col] * product
        raw[pl.ds(col, ROWS, stride=COLS), :] = after[col] * product
    for col in range(COLS):
        flat[pl.ds(col, ROWS, stride=COLS), :] = terms[col]
    put(ref, out, I0, raw[...], local)
    put(ref, out, W0, flat[...], local)


WIDE = (COLS, ROWS, CH, LANES)
TOKEN = (COLS, ROWS, LANES)
ENDS = (COLS, CH, LANES)
BLOCK = (ROWS, CH, LANES)
RATES = (COLS, ROWS, LANES)
TABLE = (COLS, 5 * ROWS, LANES)
PLACE = (COLS // 2, LANES, 256)
FLIP = (ROWS * CH, 128)


def vm(shape, kind=F32):
    return pltpu.VMEM(shape, kind)


def call(kernel, ins, outs, scratch, mebibytes, kinds=None, place=pltpu.VMEM, flops=10**8, far_in=0, far_out=0):
    near, far = pl.BlockSpec(memory_space=place), pl.BlockSpec(memory_space=pltpu.HBM)
    whole = pl.BlockSpec(memory_space=pltpu.VMEM)
    kinds = kinds or (F32,) * len(outs)
    shapes = tuple(jax.ShapeDtypeStruct(s, k) for s, k in zip(outs, kinds))
    single = len(outs) == 1
    return pl.pallas_call(
        kernel,
        out_shape=shapes[0] if single else shapes,
        in_specs=[near] * (ins - far_in) + [far] * far_in,
        out_specs=whole if single else (whole,) * (len(outs) - far_out) + (far,) * far_out,
        scratch_shapes=scratch,
        compiler_params=pltpu.CompilerParams(vmem_limit_bytes=int(mebibytes * 1024 * 1024)),
        cost_estimate=pl.CostEstimate(flops=flops, bytes_accessed=10**6, transcendentals=0),
    )


def packs():
    scratch = [vm((ROWS, COLS, SEG * CH), BF16)] * 2 + [vm((ROWS, COLS, N))] * 2
    scratch += [vm((ROWS, SEG, COLS))] * 2 + [pltpu.SemaphoreType.DMA((6,))]
    return call(pack_kernel, 6, [(SEG * SENT, 128)], scratch, 60, place=pltpu.HBM)


def edges(devices):
    outs = [(devices * EDGE, LANES), ENDS, TABLE, PLACE]
    scratch = [vm(WIDE), vm((TOKENS, LANES)), vm(RATES), vm(BLOCK), vm(FLIP, BF16)]
    return call(edges_kernel, 1, outs, scratch, 14, kinds=(F32, F32, F32, BF16))


def chains(devices):
    return call(chain_kernel, 1, [(devices, 2 * STEP, LANES)], [], 8)


def local_grads():
    outs = [(SEG * BACK, 128), (ROWS, LANES, LANES), (ROWS, LANES, LANES), WIDE, WIDE]
    scratch = [vm((COLS, 2 * LANES, 128), BF16), vm(WIDE), vm(WIDE), vm((COLS + 1,) + BLOCK), vm(ENDS)]
    scratch += [vm(BLOCK), vm(WIDE), vm((COLS, ROWS * CH, 2 * LANES), BF16), vm((4, ROWS, COLS, 8, LANES))]
    scratch += [vm(FLIP, BF16), vm((TOKENS, LANES)), vm(WIDE, BF16), pltpu.SemaphoreType.DMA((2,))]
    kinds = (F32, BF16, BF16, BF16, F32)
    return call(local_kernel, 4, outs, scratch, 50, kinds=kinds, flops=5 * 10**9, far_out=2)


def outer_grads():
    scratch = [vm(TOKEN), vm(TOKEN), vm(WIDE, BF16), vm(WIDE), vm(ENDS), vm((3, ROWS, COLS, 8, LANES)), vm(BLOCK)]
    scratch += [vm(BLOCK), vm((TOKENS, LANES)), vm((TOKENS, LANES)), vm((ROWS, LANES))]
    scratch += [pltpu.SemaphoreType.DMA((2, COLS))]
    return call(outer_kernel, 8, [(SEG * BACK, 128)], scratch, 50, far_in=2)


def unpacks():
    outs = [(ROWS, COLS, SEG * CH)] + [(ROWS, COLS, N)] * 2 + [(ROWS, SEG, COLS)] * 2
    return call(unpack_kernel, 1, outs, [], 8)


def exchange(a, axis):
    return lax.all_to_all(a.reshape(-1, 1, LANES), axis, 0, 0, tiled=True).reshape(-1, LANES)


def swapped(a):
    return jnp.transpose(a, (0, 2, 1))


def per_device(tokens, cotangent, state_in, state_out, width_decay, height_decay):
    devices = lax.axis_size("wa")
    message = packs()(
        tokens, cotangent, state_in, state_out, swapped(width_decay), swapped(height_decay)
    )
    tile = exchange(message, "ha")
    edge, back, table, place = edges(devices)(tile)
    edge = exchange(edge, "wa")
    local, high, low, *far = local_grads()(tile, back, place, table)
    carries = lax.all_to_all(chains(devices)(edge), "wa", 0, 0, tiled=True)
    answer = outer_grads()(tile, carries, local, table, high, low, *far)
    x, b, s, w, h = unpacks()(exchange(answer, "ha"))
    return x, b, s, swapped(w), swapped(h)


def solution(mesh):
    spec = P("ha", "wa", None)
    return jax.shard_map(
        per_device, mesh=mesh, in_specs=(spec,) * 6, out_specs=(spec,) * 5, check_vma=False
    )
```

```python
import jax
import jax.numpy as jnp
from jax import lax
from jax.experimental import pallas as pl
from jax.experimental.pallas import tpu as pltpu
from jax.sharding import PartitionSpec as P

F32 = jnp.float32
BF16 = jnp.bfloat16

SEG = 8
ROWS = 8
COLS = 16
CH = 64
N = 16
LANES = SEG * N
TOKENS = ROWS * COLS
STEP = 16
QUART = CH // STEP

X0, C0, B0, S0, D0 = 0, 64, 128, 144, 160
SENT = 162
I0, O0, W0 = 64, 80, 96
BACK = 98
EDGE = 33


def make_place(place):
    k = lax.broadcasted_iota(jnp.int32, (LANES, 256), 0)
    m = lax.broadcasted_iota(jnp.int32, (LANES, 256), 1)
    for two in range(COLS // 2):
        col = 2 * two + m // LANES
        hit = k == ((m % LANES) // N) * COLS + col
        place[two] = jnp.where(hit, 1.0, 0.0).astype(BF16)


def make_gather(gather):
    k = lax.broadcasted_iota(jnp.int32, (2 * LANES, 128), 0)
    m = lax.broadcasted_iota(jnp.int32, (2 * LANES, 128), 1)
    for col in range(COLS):
        hit = m == ((k % LANES) // N) * COLS + col
        gather[col] = jnp.where(hit, 1.0, 0.0).astype(BF16)


def take(ref, at, size, count):
    parts = [ref[g * count + at : g * count + at + size, :][None] for g in range(SEG)]
    return jnp.concatenate(parts, axis=0)


def give(ref, at, count, value):
    for g in range(SEG):
        ref[g * count + at : g * count + at + value.shape[1], :] = value[g]


def pack_kernel(x0, y0, b0, s0, w0, h0, out, x, y, b, s, w, h, done):
    copies = [
        pltpu.make_async_copy(source, target, done.at[k])
        for k, (source, target) in enumerate(((w0, w), (h0, h), (b0, b), (s0, s), (x0, x), (y0, y)))
    ]
    for copy in copies:
        copy.start()
    low = lax.broadcasted_iota(jnp.int32, (COLS, 128), 1) < CH
    for k, (at, a) in enumerate(((D0, w), (D0 + 1, h))):
        copies[k].wait()
        flat = jnp.concatenate([a[row] for row in range(ROWS)], axis=1)
        for g in range(SEG):
            out[g * SENT + at : g * SENT + at + 1, :] = flat[g : g + 1]
    for k, (at, a) in enumerate(((B0, b), (S0, s))):
        copies[2 + k].wait()
        flat = a[...].reshape(TOKENS, N).T
        for g in range(SEG):
            out[g * SENT + at : g * SENT + at + N, :] = flat
    for k, (at, a) in enumerate(((X0, x), (C0, y))):
        copies[4 + k].wait()
        for pair in range(ROWS // 2):
            to = at + pair * COLS
            for two in range(SEG // 2):
                lanes = slice(two * 128, (two + 1) * 128)
                one = a[2 * pair, :, lanes].astype(F32)
                other = a[2 * pair + 1, :, lanes].astype(F32)
                even, odd = 2 * two * SENT + to, (2 * two + 1) * SENT + to
                out[even : even + COLS, :] = jnp.where(low, one, pltpu.roll(other, CH, 1))
                out[odd : odd + COLS, :] = jnp.where(low, pltpu.roll(one, CH, 1), other)


def unpack_kernel(got, x, b, s, w, h):
    low = lax.broadcasted_iota(jnp.int32, (COLS, 128), 1) < CH
    for pair in range(ROWS // 2):
        for two in range(SEG // 2):
            lanes = slice(two * 128, (two + 1) * 128)
            even, odd = 2 * two * BACK + pair * COLS, (2 * two + 1) * BACK + pair * COLS
            one = got[even : even + COLS, :]
            other = got[odd : odd + COLS, :]
            x[2 * pair, :, lanes] = jnp.where(low, one, pltpu.roll(other, CH, 1))
            x[2 * pair + 1, :, lanes] = jnp.where(low, pltpu.roll(one, CH, 1), other)
    for at, a in ((I0, b), (O0, s)):
        flat = got[at : at + N, :]
        for g in range(1, SEG):
            flat = flat + got[g * BACK + at : g * BACK + at + N, :]
        a[...] = flat.T.reshape(ROWS, COLS, N)
    for at, a in ((W0, w), (W0 + 1, h)):
        flat = jnp.concatenate([got[g * BACK + at : g * BACK + at + 1, :] for g in range(SEG)], axis=0)
        for row in range(ROWS):
            a[row] = flat[:, row * COLS : (row + 1) * COLS]


def flip(ref, at, flipped):
    for pair in range(ROWS // 2):
        block = take(ref, at + pair * COLS, COLS, SENT).reshape(SEG * COLS, 2 * CH)
        flipped[pair * 2 * CH : (pair + 1) * 2 * CH, :] = block.T.astype(BF16)


def spread(flipped, place, wide, two, thin=None):
    for pair in range(ROWS // 2):
        block = flipped[pair * 2 * CH : (pair + 1) * 2 * CH, :]
        out = jnp.dot(block, place[two], preferred_element_type=F32)
        for part in range(2):
            for half in range(2):
                value = out[part * CH : (part + 1) * CH, half * LANES : (half + 1) * LANES]
                wide[2 * two + half, 2 * pair + part] = value
                if thin is not None:
                    thin[2 * two + half, 2 * pair + part] = value.astype(BF16)


def by_column(flat, out):
    for col in range(COLS):
        out[col] = flat[pl.ds(col, ROWS, stride=COLS), :]


def small(ref, flat, bt, ct, wr, hr):
    for at, out in ((B0, bt), (S0, ct)):
        flat[...] = take(ref, at, N, SENT).reshape(LANES, TOKENS).T
        by_column(flat, out)
    for at, out in ((D0, wr), (D0 + 1, hr)):
        rate = jnp.exp(take(ref, at, 1, SENT))
        flat[...] = jnp.broadcast_to(rate, (SEG, N, TOKENS)).reshape(LANES, TOKENS).T
        by_column(flat, out)


def tables(rows):
    return [rows.at[:, k * ROWS : (k + 1) * ROWS, :] for k in range(5)]


def mover(down):
    def move(v, by):
        return pltpu.roll(v, by * N if down else LANES - by * N, 1)

    return move


def inside(down):
    lane = lax.broadcasted_iota(jnp.int32, (1, LANES), 1)
    return (lane >= N) if down else (lane < LANES - N)


def carry_rates(flat, rates, down):
    move = mover(down)
    total = flat[0:COLS, :]
    for row in range(1, ROWS):
        total = total * flat[row * COLS : (row + 1) * COLS, :]
    one = jnp.where(inside(down), move(total, 1), 0.0)
    two = one * move(one, 1)
    rates[:, 0, :] = one
    rates[:, 1, :] = two
    rates[:, 2, :] = two * move(two, 2)


def carry_scan(ends, rates, down):
    move = mover(down)
    keep = inside(down)

    for part in range(2):
        cols = range(part * COLS // 2, (part + 1) * COLS // 2)
        values = [jnp.where(keep, move(ends[col], 1), 0.0) for col in cols]
        for k, by in enumerate((1, 2, 4)):
            moved = [move(f, by) for f in values]
            values = [f + rates[col, k : k + 1, :] * g for col, f, g in zip(cols, values, moved)]
        for col, f in zip(cols, values):
            ends[col] = f


def split(v):
    high = v.astype(BF16)
    return high, (v - high.astype(F32)).astype(BF16)


def own_segment():
    r = lax.broadcasted_iota(jnp.int32, (LANES, LANES), 0)
    m = lax.broadcasted_iota(jnp.int32, (LANES, LANES), 1)
    return r // COLS == m // N


def diagonal(flat, row, own):
    value = flat[pl.ds(row, COLS, stride=ROWS), :]
    return jnp.where(own, jnp.concatenate([value] * SEG, axis=0), 0.0)


def edges_kernel(ref, edge, back, rows, place, ce, flat, rates, head, flipped):
    make_place(place)
    bt, ct, wr, hr, down = tables(rows)
    small(ref, flat, bt, ct, wr, hr)
    carry_rates(flat, rates, False)
    carry_rates(flat, down, True)
    flip(ref, C0, flipped)
    for two in range(COLS // 2):
        spread(flipped, place, ce, two)

    def ends(step, none):
        cols = [step * 4 + k for k in range(4)]
        carries = [jnp.zeros((CH, LANES), F32)] * 4
        for row in reversed(range(ROWS)):
            one = slice(row, row + 1)
            seeded = [ct[c, one, :] * ce[c, row] for c in cols]
            for c, v in zip(cols, seeded):
                ce[c, row] = v
            carries = [hr[c, one, :] * (v + seed) for c, v, seed in zip(cols, carries, seeded)]
        for c, v in zip(cols, carries):
            back[c] = v
        return none

    lax.fori_loop(0, COLS // 4, ends, 0)
    carry_scan(back, rates, False)

    after = jnp.ones((ROWS, LANES), F32)
    for col in reversed(range(COLS)):
        flat[col * ROWS : (col + 1) * ROWS, :] = after * bt[col]
        after = after * wr[col]
    own = own_segment()
    flip(ref, X0, flipped)
    for pair in range(ROWS // 2):
        for part in range(2):
            row = 2 * pair + part
            high, low = split(diagonal(flat, row, own))
            mine = flipped[row * CH : (row + 1) * CH, :]
            tail = jnp.dot(mine, high, preferred_element_type=F32) + jnp.dot(
                mine, low, preferred_element_type=F32
            )
            for q in range(QUART):
                at = (row * QUART + q) * EDGE
                edge[at : at + STEP, :] = tail[q * STEP : (q + 1) * STEP]
                edge[at + 2 * STEP : at + EDGE, :] = after[row : row + 1]

    head[...] = jnp.zeros_like(head)

    def sums(step, none):
        col = COLS - 1 - 2 * step
        carry, carry2 = back[col], back[col - 1]
        for row in reversed(range(ROWS)):
            one = slice(row, row + 1)
            grad = carry + ce[col, row]
            carry = hr[col, one, :] * grad
            grad2 = carry2 + ce[col - 1, row]
            carry2 = hr[col - 1, one, :] * grad2
            head[row] = wr[col - 1, one, :] * (wr[col, one, :] * (head[row] + grad) + grad2)
        return none

    lax.fori_loop(0, COLS // 2, sums, 0)
    for row in range(ROWS):
        for q in range(QUART):
            at = (row * QUART + q) * EDGE + STEP
            edge[at : at + STEP, :] = head[row, q * STEP : (q + 1) * STEP, :]


def chain_kernel(got, out):
    count = out.shape[0]
    right = left = jnp.zeros((STEP, LANES), F32)
    for hop in range(count):
        place = count - 1 - hop
        out[hop, 0:STEP, :] = right
        out[place, STEP : 2 * STEP, :] = left
        one, other = hop * EDGE, place * EDGE
        right = got[one + 2 * STEP : one + EDGE, :] * right + got[one : one + STEP, :]
        left = got[other + 2 * STEP : other + EDGE, :] * left + got[other + STEP : other + 2 * STEP, :]


def total8(v):
    v = v[0 : CH // 2] + v[CH // 2 :]
    v = v[0 : CH // 4] + v[CH // 4 :]
    return v[0:8] + v[8:16]


def local_kernel(
    ref, back, place, table, out, high, low, far_ce, far_grad,
    gather, xe, ce, states, front, run, kept, pieces, sums, flipped, flat, thin, done
):
    bt, ct, wr, hr, rates = tables(table)
    make_gather(gather)
    value = jnp.ones((ROWS, LANES), F32)
    for col in reversed(range(COLS)):
        flat[col * ROWS : (col + 1) * ROWS, :] = value * bt[col]
        value = value * wr[col]
    own = own_segment()
    for row in range(ROWS):
        high[row], low[row] = split(diagonal(flat, row, own))
    flip(ref, X0, flipped)
    for two in range(COLS // 2):
        spread(flipped, place, xe, two)
    flip(ref, C0, flipped)
    for two in range(COLS // 2):
        spread(flipped, place, ce, two, thin)
    copies = [
        pltpu.make_async_copy(source, target, done.at[k])
        for k, (source, target) in enumerate(((thin, far_ce), (kept, far_grad)))
    ]
    copies[0].start()
    states[0] = jnp.zeros(BLOCK, F32)
    run[...] = jnp.zeros(BLOCK, F32)

    def forward(col, none):
        total = jnp.zeros((CH, LANES), F32)
        for row in range(ROWS):
            one = slice(row, row + 1)
            state = wr[col, one, :] * states[col, row] + bt[col, one, :] * xe[col, row]
            states[col + 1, row] = state
            total = hr[col, one, :] * total + state
        front[col] = total
        return none

    lax.fori_loop(0, COLS, forward, 0)
    carry_scan(front, rates, True)

    def products(step, none):
        col = COLS - 1 - step
        carry = back[col]
        for row in reversed(range(ROWS)):
            one = slice(row, row + 1)
            grad = carry + ct[col, one, :] * ce[col, row]
            carry = hr[col, one, :] * grad
            kept[col, row] = grad
        total = front[col]
        for row in range(ROWS):
            one = slice(row, row + 1)
            grad = kept[col, row]
            sums[3, row, col] = total8(grad * total)
            total = hr[col, one, :] * total + states[col + 1, row]
            sums[1, row, col] = total8(total * ce[col, row])
            grad = grad + run[row]
            run[row] = wr[col, one, :] * grad
            sums[2, row, col] = total8(grad * states[col, row])
            sums[0, row, col] = total8(grad * xe[col, row])
            high, low = split(grad * bt[col, one, :])
            pieces[col, row * CH : (row + 1) * CH, 0:LANES] = high
            pieces[col, row * CH : (row + 1) * CH, LANES:] = low
        return none

    lax.fori_loop(0, COLS, products, 0)
    copies[1].start()
    for pair in range(ROWS // 2):
        rows = slice(pair * 2 * CH, (pair + 1) * 2 * CH)
        block = jnp.zeros((2 * CH, 128), F32)
        for col in range(COLS):
            block = block + jnp.dot(pieces[col, rows, :], gather[col], preferred_element_type=F32)
        give(out, pair * COLS, BACK, block.T.reshape(SEG, COLS, 2 * CH))
    for which, at in enumerate((I0, O0, W0, W0 + 1)):
        put(ref, out, at, over_sublanes(sums.at[which]))
    for copy in copies:
        copy.wait()


def over_sublanes(part):
    rows = part.reshape(TOKENS * 8, LANES)
    value = rows[pl.ds(0, TOKENS, stride=8), :]
    for k in range(1, 8):
        value = value + rows[pl.ds(k, TOKENS, stride=8), :]
    return value


def put(ref, out, at, value, old=None):
    value = value.T.reshape(SEG, N, TOKENS)
    size = N
    if at >= W0:
        rate = jnp.exp(take(ref, D0 + at - W0, 1, SENT))
        value, size = rate * jnp.sum(value, axis=1, keepdims=True), 1
    if old is not None:
        value = value + take(old, at, size, BACK)
    give(out, at, BACK, value)


def outer_kernel(
    ref, edge, local, table, high, low, far_ce, far_grad, out,
    before, after, ce, inner, front, sums, left, right, flat, raw, meet, entered, done
):
    def fetch(col):
        return (
            pltpu.make_async_copy(far_grad.at[col], inner.at[col], done.at[0, col]),
            pltpu.make_async_copy(far_ce.at[col], ce.at[col], done.at[1, col]),
        )

    for col in range(COLS):
        for copy in fetch(col):
            copy.start()
    bt, ct, wr, hr, rates = tables(table)
    value = jnp.ones((ROWS, LANES), F32)
    for col in range(COLS):
        value = value * wr[col]
        before[col] = value
    value = jnp.ones((ROWS, LANES), F32)
    for col in reversed(range(COLS)):
        after[col] = value
        value = value * wr[col]
    for row in range(ROWS):
        for q in range(QUART):
            part = slice(q * STEP, (q + 1) * STEP)
            left[row, part, :] = edge[row * QUART + q, 0:STEP, :]
            right[row, part, :] = edge[row * QUART + q, STEP : 2 * STEP, :]

    own = own_segment()
    empty = jnp.zeros((CH, LANES), BF16)
    half = lax.broadcasted_iota(jnp.int32, (LANES, 128), 1) < CH
    for pair in range(ROWS // 2):
        tokens = take(ref, X0 + pair * COLS, COLS, SENT).reshape(SEG * COLS, 2 * CH).astype(BF16)
        parts = [split(right[2 * pair + part]) for part in range(2)]
        both = [jnp.concatenate([parts[0][k], parts[1][k]], axis=0) for k in range(2)]
        found = []
        for part in range(2):
            row = 2 * pair + part
            value = jnp.zeros((LANES, LANES), F32)
            for k in range(2):
                pieces = [parts[0][k], empty] if part == 0 else [empty, parts[1][k]]
                value = value + jnp.dot(tokens, jnp.concatenate(pieces, axis=0), preferred_element_type=F32)
            value = jnp.where(own, value, 0.0).reshape(SEG, COLS, LANES)
            raw[row * COLS : (row + 1) * COLS, :] = jnp.sum(value, axis=0)
            meet[row : row + 1, :] = jnp.sum(right[row] * left[row], axis=0, keepdims=True)
            value = jnp.zeros((LANES, 128), F32)
            for weight, k in ((low, 0), (high, 1), (high, 0)):
                value = value + lax.dot_general(
                    weight[row], both[k], (((1,), (1,)), ((), ())), preferred_element_type=F32
                )
            found.append(value)
        value = jnp.where(half, found[0], found[1]).reshape(SEG, COLS, 128)
        give(out, pair * COLS, BACK, take(local, pair * COLS, COLS, BACK) + value)

    def forward(step, none):
        cols = [step * 4 + k for k in range(4)]
        totals = [jnp.zeros((CH, LANES), F32)] * 4
        for row in range(ROWS):
            one = slice(row, row + 1)
            enter = left[row]
            parts = [before[c, one, :] * enter for c in cols]
            for c, v in zip(cols, parts):
                entered[c, row] = v
            totals = [hr[c, one, :] * v + part for c, v, part in zip(cols, totals, parts)]
        for c, v in zip(cols, totals):
            front[c] = v
        return none

    lax.fori_loop(0, COLS // 4, forward, 0)
    carry_scan(front, rates, True)

    def products(col, none):
        for copy in fetch(col):
            copy.wait()
        total = front[col]
        for row in range(ROWS):
            one = slice(row, row + 1)
            grad = inner[col, row]
            sums[2, row, col] = total8(grad * left[row])
            sums[1, row, col] = total8(grad * total)
            total = hr[col, one, :] * total + entered[col, row]
            sums[0, row, col] = total8(total * ce[col, row].astype(F32))
        return none

    lax.fori_loop(0, COLS, products, 0)

    put(ref, out, O0, over_sublanes(sums.at[0]), local)
    put(ref, out, W0 + 1, over_sublanes(sums.at[1]), local)
    flat[...] = over_sublanes(sums.at[2])

    def rows_of(a, col):
        return a[pl.ds(col, ROWS, stride=COLS), :]

    value = jnp.zeros((ROWS, LANES), F32)
    terms = [None] * COLS
    for col in reversed(range(COLS)):
        value = rows_of(flat, col) + value
        terms[col] = value * before[col - 1] if col else value
        value = wr[col] * value
    value = meet[...]
    for col in range(COLS):
        terms[col] = terms[col] + after[col] * value
        product = rows_of(raw, col)
        value = wr[col] * value + bt[col] * product
        raw[pl.ds(col, ROWS, stride=COLS), :] = after[col] * product
    for col in range(COLS):
        flat[pl.ds(col, ROWS, stride=COLS), :] = terms[col]
    put(ref, out, I0, raw[...], local)
    put(ref, out, W0, flat[...], local)


WIDE = (COLS, ROWS, CH, LANES)
TOKEN = (COLS, ROWS, LANES)
ENDS = (COLS, CH, LANES)
BLOCK = (ROWS, CH, LANES)
RATES = (COLS, ROWS, LANES)
TABLE = (COLS, 5 * ROWS, LANES)
PLACE = (COLS // 2, LANES, 256)
FLIP = (ROWS * CH, 128)


def vm(shape, kind=F32):
    return pltpu.VMEM(shape, kind)


def call(kernel, ins, outs, scratch, mebibytes, kinds=None, place=pltpu.VMEM, flops=10**8, far_in=0, far_out=0):
    near, far = pl.BlockSpec(memory_space=place), pl.BlockSpec(memory_space=pltpu.HBM)
    whole = pl.BlockSpec(memory_space=pltpu.VMEM)
    kinds = kinds or (F32,) * len(outs)
    shapes = tuple(jax.ShapeDtypeStruct(s, k) for s, k in zip(outs, kinds))
    single = len(outs) == 1
    return pl.pallas_call(
        kernel,
        out_shape=shapes[0] if single else shapes,
        in_specs=[near] * (ins - far_in) + [far] * far_in,
        out_specs=whole if single else (whole,) * (len(outs) - far_out) + (far,) * far_out,
        scratch_shapes=scratch,
        compiler_params=pltpu.CompilerParams(vmem_limit_bytes=int(mebibytes * 1024 * 1024)),
        cost_estimate=pl.CostEstimate(flops=flops, bytes_accessed=10**6, transcendentals=0),
    )


def packs():
    scratch = [vm((ROWS, COLS, SEG * CH), BF16)] * 2 + [vm((ROWS, COLS, N))] * 2
    scratch += [vm((ROWS, SEG, COLS))] * 2 + [pltpu.SemaphoreType.DMA((6,))]
    return call(pack_kernel, 6, [(SEG * SENT, 128)], scratch, 60, place=pltpu.HBM)


def edges(devices):
    outs = [(devices * EDGE, LANES), ENDS, TABLE, PLACE]
    scratch = [vm(WIDE), vm((TOKENS, LANES)), vm(RATES), vm(BLOCK), vm(FLIP, BF16)]
    return call(edges_kernel, 1, outs, scratch, 14, kinds=(F32, F32, F32, BF16))


def chains(devices):
    return call(chain_kernel, 1, [(devices, 2 * STEP, LANES)], [], 8)


def local_grads():
    outs = [(SEG * BACK, 128), (ROWS, LANES, LANES), (ROWS, LANES, LANES), WIDE, WIDE]
    scratch = [vm((COLS, 2 * LANES, 128), BF16), vm(WIDE), vm(WIDE), vm((COLS + 1,) + BLOCK), vm(ENDS)]
    scratch += [vm(BLOCK), vm(WIDE), vm((COLS, ROWS * CH, 2 * LANES), BF16), vm((4, ROWS, COLS, 8, LANES))]
    scratch += [vm(FLIP, BF16), vm((TOKENS, LANES)), vm(WIDE, BF16), pltpu.SemaphoreType.DMA((2,))]
    kinds = (F32, BF16, BF16, BF16, F32)
    return call(local_kernel, 4, outs, scratch, 50, kinds=kinds, flops=5 * 10**9, far_out=2)


def outer_grads():
    scratch = [vm(TOKEN), vm(TOKEN), vm(WIDE, BF16), vm(WIDE), vm(ENDS), vm((3, ROWS, COLS, 8, LANES)), vm(BLOCK)]
    scratch += [vm(BLOCK), vm((TOKENS, LANES)), vm((TOKENS, LANES)), vm((ROWS, LANES))]
    scratch += [vm(WIDE), pltpu.SemaphoreType.DMA((2, COLS))]
    return call(outer_kernel, 8, [(SEG * BACK, 128)], scratch, 50, far_in=2)


def unpacks():
    outs = [(ROWS, COLS, SEG * CH)] + [(ROWS, COLS, N)] * 2 + [(ROWS, SEG, COLS)] * 2
    return call(unpack_kernel, 1, outs, [], 8)


def exchange(a, axis):
    return lax.all_to_all(a.reshape(-1, 1, LANES), axis, 0, 0, tiled=True).reshape(-1, LANES)


def swapped(a):
    return jnp.transpose(a, (0, 2, 1))


def per_device(tokens, cotangent, state_in, state_out, width_decay, height_decay):
    devices = lax.axis_size("wa")
    message = packs()(
        tokens, cotangent, state_in, state_out, swapped(width_decay), swapped(height_decay)
    )
    tile = exchange(message, "ha")
    edge, back, table, place = edges(devices)(tile)
    edge = exchange(edge, "wa")
    local, high, low, *far = local_grads()(tile, back, place, table)
    carries = lax.all_to_all(chains(devices)(edge), "wa", 0, 0, tiled=True)
    answer = outer_grads()(tile, carries, local, table, high, low, *far)
    x, b, s, w, h = unpacks()(exchange(answer, "ha"))
    return x, b, s, swapped(w), swapped(h)


def solution(mesh):
    spec = P("ha", "wa", None)
    return jax.shard_map(
        per_device, mesh=mesh, in_specs=(spec,) * 6, out_specs=(spec,) * 5, check_vma=False
    )
```

```python
import jax
import jax.numpy as jnp
from jax import lax
from jax.experimental import pallas as pl
from jax.experimental.pallas import tpu as pltpu
from jax.sharding import PartitionSpec as P

F32 = jnp.float32
BF16 = jnp.bfloat16

SEG = 8
ROWS = 8
COLS = 16
CH = 64
N = 16
LANES = SEG * N
TOKENS = ROWS * COLS
STEP = 16
QUART = CH // STEP

X0, C0, B0, S0, D0 = 0, 64, 128, 144, 160
SENT = 162
I0, O0, W0 = 64, 80, 96
BACK = 98
EDGE = 33


def make_place(place):
    k = lax.broadcasted_iota(jnp.int32, (LANES, 256), 0)
    m = lax.broadcasted_iota(jnp.int32, (LANES, 256), 1)
    for two in range(COLS // 2):
        col = 2 * two + m // LANES
        hit = k == ((m % LANES) // N) * COLS + col
        place[two] = jnp.where(hit, 1.0, 0.0).astype(BF16)


def make_gather(gather):
    k = lax.broadcasted_iota(jnp.int32, (2 * LANES, 128), 0)
    m = lax.broadcasted_iota(jnp.int32, (2 * LANES, 128), 1)
    for col in range(COLS):
        hit = m == ((k % LANES) // N) * COLS + col
        gather[col] = jnp.where(hit, 1.0, 0.0).astype(BF16)


def take(ref, at, size, count):
    parts = [ref[g * count + at : g * count + at + size, :][None] for g in range(SEG)]
    return jnp.concatenate(parts, axis=0)


def give(ref, at, count, value):
    for g in range(SEG):
        ref[g * count + at : g * count + at + value.shape[1], :] = value[g]


def pack_kernel(x0, y0, b0, s0, w0, h0, out, x, y, b, s, w, h, done):
    copies = [
        pltpu.make_async_copy(source, target, done.at[k])
        for k, (source, target) in enumerate(((w0, w), (h0, h), (b0, b), (s0, s), (x0, x), (y0, y)))
    ]
    for copy in copies:
        copy.start()
    low = lax.broadcasted_iota(jnp.int32, (COLS, 128), 1) < CH
    for k, (at, a) in enumerate(((D0, w), (D0 + 1, h))):
        copies[k].wait()
        flat = jnp.concatenate([a[row] for row in range(ROWS)], axis=1)
        for g in range(SEG):
            out[g * SENT + at : g * SENT + at + 1, :] = flat[g : g + 1]
    for k, (at, a) in enumerate(((B0, b), (S0, s))):
        copies[2 + k].wait()
        flat = a[...].reshape(TOKENS, N).T
        for g in range(SEG):
            out[g * SENT + at : g * SENT + at + N, :] = flat
    for k, (at, a) in enumerate(((X0, x), (C0, y))):
        copies[4 + k].wait()
        for pair in range(ROWS // 2):
            to = at + pair * COLS
            for two in range(SEG // 2):
                lanes = slice(two * 128, (two + 1) * 128)
                one = a[2 * pair, :, lanes].astype(F32)
                other = a[2 * pair + 1, :, lanes].astype(F32)
                even, odd = 2 * two * SENT + to, (2 * two + 1) * SENT + to
                out[even : even + COLS, :] = jnp.where(low, one, pltpu.roll(other, CH, 1))
                out[odd : odd + COLS, :] = jnp.where(low, pltpu.roll(one, CH, 1), other)


def unpack_kernel(got, x, b, s, w, h):
    low = lax.broadcasted_iota(jnp.int32, (COLS, 128), 1) < CH
    for pair in range(ROWS // 2):
        for two in range(SEG // 2):
            lanes = slice(two * 128, (two + 1) * 128)
            even, odd = 2 * two * BACK + pair * COLS, (2 * two + 1) * BACK + pair * COLS
            one = got[even : even + COLS, :]
            other = got[odd : odd + COLS, :]
            x[2 * pair, :, lanes] = jnp.where(low, one, pltpu.roll(other, CH, 1))
            x[2 * pair + 1, :, lanes] = jnp.where(low, pltpu.roll(one, CH, 1), other)
    for at, a in ((I0, b), (O0, s)):
        flat = got[at : at + N, :]
        for g in range(1, SEG):
            flat = flat + got[g * BACK + at : g * BACK + at + N, :]
        a[...] = flat.T.reshape(ROWS, COLS, N)
    for at, a in ((W0, w), (W0 + 1, h)):
        flat = jnp.concatenate([got[g * BACK + at : g * BACK + at + 1, :] for g in range(SEG)], axis=0)
        for row in range(ROWS):
            a[row] = flat[:, row * COLS : (row + 1) * COLS]


def flip(ref, at, flipped):
    for pair in range(ROWS // 2):
        block = take(ref, at + pair * COLS, COLS, SENT).reshape(SEG * COLS, 2 * CH)
        flipped[pair * 2 * CH : (pair + 1) * 2 * CH, :] = block.T.astype(BF16)


def spread(flipped, place, wide, two, thin=None):
    for pair in range(ROWS // 2):
        block = flipped[pair * 2 * CH : (pair + 1) * 2 * CH, :]
        out = jnp.dot(block, place[two], preferred_element_type=F32)
        for part in range(2):
            for half in range(2):
                value = out[part * CH : (part + 1) * CH, half * LANES : (half + 1) * LANES]
                wide[2 * two + half, 2 * pair + part] = value
                if thin is not None:
                    thin[2 * two + half, 2 * pair + part] = value.astype(BF16)


def by_column(flat, out):
    for col in range(COLS):
        out[col] = flat[pl.ds(col, ROWS, stride=COLS), :]


def small(ref, flat, bt, ct, wr, hr):
    for at, out in ((B0, bt), (S0, ct)):
        flat[...] = take(ref, at, N, SENT).reshape(LANES, TOKENS).T
        by_column(flat, out)
    for at, out in ((D0, wr), (D0 + 1, hr)):
        rate = jnp.exp(take(ref, at, 1, SENT))
        flat[...] = jnp.broadcast_to(rate, (SEG, N, TOKENS)).reshape(LANES, TOKENS).T
        by_column(flat, out)


def tables(rows):
    return [rows.at[:, k * ROWS : (k + 1) * ROWS, :] for k in range(5)]


def mover(down):
    def move(v, by):
        return pltpu.roll(v, by * N if down else LANES - by * N, 1)

    return move


def inside(down):
    lane = lax.broadcasted_iota(jnp.int32, (1, LANES), 1)
    return (lane >= N) if down else (lane < LANES - N)


def carry_rates(flat, rates, down):
    move = mover(down)
    total = flat[0:COLS, :]
    for row in range(1, ROWS):
        total = total * flat[row * COLS : (row + 1) * COLS, :]
    one = jnp.where(inside(down), move(total, 1), 0.0)
    two = one * move(one, 1)
    rates[:, 0, :] = one
    rates[:, 1, :] = two
    rates[:, 2, :] = two * move(two, 2)


def carry_scan(ends, rates, down):
    move = mover(down)
    keep = inside(down)

    for part in range(1):
        cols = range(COLS)
        values = [jnp.where(keep, move(ends[col], 1), 0.0) for col in cols]
        for k, by in enumerate((1, 2, 4)):
            moved = [move(f, by) for f in values]
            values = [f + rates[col, k : k + 1, :] * g for col, f, g in zip(cols, values, moved)]
        for col, f in zip(cols, values):
            ends[col] = f


def split(v):
    high = v.astype(BF16)
    return high, (v - high.astype(F32)).astype(BF16)


def own_segment():
    r = lax.broadcasted_iota(jnp.int32, (LANES, LANES), 0)
    m = lax.broadcasted_iota(jnp.int32, (LANES, LANES), 1)
    return r // COLS == m // N


def diagonal(flat, row, own):
    value = flat[pl.ds(row, COLS, stride=ROWS), :]
    return jnp.where(own, jnp.concatenate([value] * SEG, axis=0), 0.0)


def edges_kernel(ref, edge, back, rows, place, ce, flat, rates, head, flipped):
    make_place(place)
    bt, ct, wr, hr, down = tables(rows)
    small(ref, flat, bt, ct, wr, hr)
    carry_rates(flat, rates, False)
    carry_rates(flat, down, True)
    flip(ref, C0, flipped)
    for two in range(COLS // 2):
        spread(flipped, place, ce, two)

    def ends(step, none):
        cols = [step * 4 + k for k in range(4)]
        carries = [jnp.zeros((CH, LANES), F32)] * 4
        for row in reversed(range(ROWS)):
            one = slice(row, row + 1)
            carries = [hr[c, one, :] * (v + ct[c, one, :] * ce[c, row]) for c, v in zip(cols, carries)]
        for c, v in zip(cols, carries):
            back[c] = v
        return none

    lax.fori_loop(0, COLS // 4, ends, 0)
    carry_scan(back, rates, False)

    after = jnp.ones((ROWS, LANES), F32)
    for col in reversed(range(COLS)):
        flat[col * ROWS : (col + 1) * ROWS, :] = after * bt[col]
        after = after * wr[col]
    own = own_segment()
    flip(ref, X0, flipped)
    for pair in range(ROWS // 2):
        for part in range(2):
            row = 2 * pair + part
            high, low = split(diagonal(flat, row, own))
            mine = flipped[row * CH : (row + 1) * CH, :]
            tail = jnp.dot(mine, high, preferred_element_type=F32) + jnp.dot(
                mine, low, preferred_element_type=F32
            )
            for q in range(QUART):
                at = (row * QUART + q) * EDGE
                edge[at : at + STEP, :] = tail[q * STEP : (q + 1) * STEP]
                edge[at + 2 * STEP : at + EDGE, :] = after[row : row + 1]

    head[...] = jnp.zeros_like(head)

    def sums(step, none):
        col = COLS - 1 - 2 * step
        carry, carry2 = back[col], back[col - 1]
        for row in reversed(range(ROWS)):
            one = slice(row, row + 1)
            grad = carry + ct[col, one, :] * ce[col, row]
            carry = hr[col, one, :] * grad
            grad2 = carry2 + ct[col - 1, one, :] * ce[col - 1, row]
            carry2 = hr[col - 1, one, :] * grad2
            head[row] = wr[col - 1, one, :] * (wr[col, one, :] * (head[row] + grad) + grad2)
        return none

    lax.fori_loop(0, COLS // 2, sums, 0)
    for row in range(ROWS):
        for q in range(QUART):
            at = (row * QUART + q) * EDGE + STEP
            edge[at : at + STEP, :] = head[row, q * STEP : (q + 1) * STEP, :]


def chain_kernel(got, out):
    count = out.shape[0]
    right = left = jnp.zeros((STEP, LANES), F32)
    for hop in range(count):
        place = count - 1 - hop
        out[hop, 0:STEP, :] = right
        out[place, STEP : 2 * STEP, :] = left
        one, other = hop * EDGE, place * EDGE
        right = got[one + 2 * STEP : one + EDGE, :] * right + got[one : one + STEP, :]
        left = got[other + 2 * STEP : other + EDGE, :] * left + got[other + STEP : other + 2 * STEP, :]


def total8(v):
    v = v[0 : CH // 2] + v[CH // 2 :]
    v = v[0 : CH // 4] + v[CH // 4 :]
    return v[0:8] + v[8:16]


def local_kernel(
    ref, back, place, table, out, high, low, far_ce, far_grad,
    gather, xe, ce, states, front, run, kept, pieces, sums, flipped, flat, thin, done
):
    bt, ct, wr, hr, rates = tables(table)
    make_gather(gather)
    value = jnp.ones((ROWS, LANES), F32)
    for col in reversed(range(COLS)):
        flat[col * ROWS : (col + 1) * ROWS, :] = value * bt[col]
        value = value * wr[col]
    own = own_segment()
    for row in range(ROWS):
        high[row], low[row] = split(diagonal(flat, row, own))
    flip(ref, X0, flipped)
    for two in range(COLS // 2):
        spread(flipped, place, xe, two)
    flip(ref, C0, flipped)
    for two in range(COLS // 2):
        spread(flipped, place, ce, two, thin)
    copies = [
        pltpu.make_async_copy(source, target, done.at[k])
        for k, (source, target) in enumerate(((thin, far_ce), (kept, far_grad)))
    ]
    copies[0].start()
    states[0] = jnp.zeros(BLOCK, F32)
    run[...] = jnp.zeros(BLOCK, F32)

    def forward(col, none):
        total = jnp.zeros((CH, LANES), F32)
        for row in range(ROWS):
            one = slice(row, row + 1)
            state = wr[col, one, :] * states[col, row] + bt[col, one, :] * xe[col, row]
            states[col + 1, row] = state
            total = hr[col, one, :] * total + state
        front[col] = total
        return none

    lax.fori_loop(0, COLS, forward, 0)
    carry_scan(front, rates, True)

    def products(step, none):
        col = COLS - 1 - step
        carry = back[col]
        for row in reversed(range(ROWS)):
            one = slice(row, row + 1)
            grad = carry + ct[col, one, :] * ce[col, row]
            carry = hr[col, one, :] * grad
            kept[col, row] = grad
        total = front[col]
        for row in range(ROWS):
            one = slice(row, row + 1)
            grad = kept[col, row]
            sums[3, row, col] = total8(grad * total)
            total = hr[col, one, :] * total + states[col + 1, row]
            sums[1, row, col] = total8(total * ce[col, row])
            grad = grad + run[row]
            run[row] = wr[col, one, :] * grad
            sums[2, row, col] = total8(grad * states[col, row])
            sums[0, row, col] = total8(grad * xe[col, row])
            high, low = split(grad * bt[col, one, :])
            pieces[col, row * CH : (row + 1) * CH, 0:LANES] = high
            pieces[col, row * CH : (row + 1) * CH, LANES:] = low
        return none

    lax.fori_loop(0, COLS, products, 0)
    copies[1].start()
    for pair in range(ROWS // 2):
        rows = slice(pair * 2 * CH, (pair + 1) * 2 * CH)
        block = jnp.zeros((2 * CH, 128), F32)
        for col in range(COLS):
            block = block + jnp.dot(pieces[col, rows, :], gather[col], preferred_element_type=F32)
        give(out, pair * COLS, BACK, block.T.reshape(SEG, COLS, 2 * CH))
    for which, at in enumerate((I0, O0, W0, W0 + 1)):
        put(ref, out, at, over_sublanes(sums.at[which]))
    for copy in copies:
        copy.wait()


def over_sublanes(part):
    rows = part.reshape(TOKENS * 8, LANES)
    value = rows[pl.ds(0, TOKENS, stride=8), :]
    for k in range(1, 8):
        value = value + rows[pl.ds(k, TOKENS, stride=8), :]
    return value


def put(ref, out, at, value, old=None):
    value = value.T.reshape(SEG, N, TOKENS)
    size = N
    if at >= W0:
        rate = jnp.exp(take(ref, D0 + at - W0, 1, SENT))
        value, size = rate * jnp.sum(value, axis=1, keepdims=True), 1
    if old is not None:
        value = value + take(old, at, size, BACK)
    give(out, at, BACK, value)


def outer_kernel(
    ref, edge, local, table, high, low, far_ce, far_grad, out,
    before, after, ce, inner, front, sums, left, right, flat, raw, meet, done
):
    def fetch(col):
        return (
            pltpu.make_async_copy(far_grad.at[col], inner.at[col], done.at[0, col]),
            pltpu.make_async_copy(far_ce.at[col], ce.at[col], done.at[1, col]),
        )

    for col in range(COLS):
        for copy in fetch(col):
            copy.start()
    bt, ct, wr, hr, rates = tables(table)
    value = jnp.ones((ROWS, LANES), F32)
    for col in range(COLS):
        value = value * wr[col]
        before[col] = value
    value = jnp.ones((ROWS, LANES), F32)
    for col in reversed(range(COLS)):
        after[col] = value
        value = value * wr[col]
    for row in range(ROWS):
        for q in range(QUART):
            part = slice(q * STEP, (q + 1) * STEP)
            left[row, part, :] = edge[row * QUART + q, 0:STEP, :]
            right[row, part, :] = edge[row * QUART + q, STEP : 2 * STEP, :]

    own = own_segment()
    empty = jnp.zeros((CH, LANES), BF16)
    half = lax.broadcasted_iota(jnp.int32, (LANES, 128), 1) < CH
    for pair in range(ROWS // 2):
        tokens = take(ref, X0 + pair * COLS, COLS, SENT).reshape(SEG * COLS, 2 * CH).astype(BF16)
        parts = [split(right[2 * pair + part]) for part in range(2)]
        both = [jnp.concatenate([parts[0][k], parts[1][k]], axis=0) for k in range(2)]
        found = []
        for part in range(2):
            row = 2 * pair + part
            value = jnp.zeros((LANES, LANES), F32)
            for k in range(2):
                pieces = [parts[0][k], empty] if part == 0 else [empty, parts[1][k]]
                value = value + jnp.dot(tokens, jnp.concatenate(pieces, axis=0), preferred_element_type=F32)
            value = jnp.where(own, value, 0.0).reshape(SEG, COLS, LANES)
            raw[row * COLS : (row + 1) * COLS, :] = jnp.sum(value, axis=0)
            meet[row : row + 1, :] = jnp.sum(right[row] * left[row], axis=0, keepdims=True)
            value = jnp.zeros((LANES, 128), F32)
            for weight, k in ((low, 0), (high, 1), (high, 0)):
                value = value + lax.dot_general(
                    weight[row], both[k], (((1,), (1,)), ((), ())), preferred_element_type=F32
                )
            found.append(value)
        value = jnp.where(half, found[0], found[1]).reshape(SEG, COLS, 128)
        give(out, pair * COLS, BACK, take(local, pair * COLS, COLS, BACK) + value)

    def forward(step, none):
        cols = [step * 4 + k for k in range(4)]
        totals = [jnp.zeros((CH, LANES), F32)] * 4
        for row in range(ROWS):
            one = slice(row, row + 1)
            enter = left[row]
            totals = [hr[c, one, :] * v + before[c, one, :] * enter for c, v in zip(cols, totals)]
        for c, v in zip(cols, totals):
            front[c] = v
        return none

    lax.fori_loop(0, COLS // 4, forward, 0)
    carry_scan(front, rates, True)

    def products(col, none):
        for copy in fetch(col):
            copy.wait()
        total = front[col]
        for row in range(ROWS):
            one = slice(row, row + 1)
            grad = inner[col, row]
            sums[2, row, col] = total8(grad * left[row])
            sums[1, row, col] = total8(grad * total)
            total = hr[col, one, :] * total + before[col, one, :] * left[row]
            sums[0, row, col] = total8(total * ce[col, row].astype(F32))
        return none

    lax.fori_loop(0, COLS, products, 0)

    put(ref, out, O0, over_sublanes(sums.at[0]), local)
    put(ref, out, W0 + 1, over_sublanes(sums.at[1]), local)
    flat[...] = over_sublanes(sums.at[2])

    def rows_of(a, col):
        return a[pl.ds(col, ROWS, stride=COLS), :]

    value = jnp.zeros((ROWS, LANES), F32)
    terms = [None] * COLS
    for col in reversed(range(COLS)):
        value = rows_of(flat, col) + value
        terms[col] = value * before[col - 1] if col else value
        value = wr[col] * value
    value = meet[...]
    for col in range(COLS):
        terms[col] = terms[col] + after[col] * value
        product = rows_of(raw, col)
        value = wr[col] * value + bt[col] * product
        raw[pl.ds(col, ROWS, stride=COLS), :] = after[col] * product
    for col in range(COLS):
        flat[pl.ds(col, ROWS, stride=COLS), :] = terms[col]
    put(ref, out, I0, raw[...], local)
    put(ref, out, W0, flat[...], local)


WIDE = (COLS, ROWS, CH, LANES)
TOKEN = (COLS, ROWS, LANES)
ENDS = (COLS, CH, LANES)
BLOCK = (ROWS, CH, LANES)
RATES = (COLS, ROWS, LANES)
TABLE = (COLS, 5 * ROWS, LANES)
PLACE = (COLS // 2, LANES, 256)
FLIP = (ROWS * CH, 128)


def vm(shape, kind=F32):
    return pltpu.VMEM(shape, kind)


def call(kernel, ins, outs, scratch, mebibytes, kinds=None, place=pltpu.VMEM, flops=10**8, far_in=0, far_out=0):
    near, far = pl.BlockSpec(memory_space=place), pl.BlockSpec(memory_space=pltpu.HBM)
    whole = pl.BlockSpec(memory_space=pltpu.VMEM)
    kinds = kinds or (F32,) * len(outs)
    shapes = tuple(jax.ShapeDtypeStruct(s, k) for s, k in zip(outs, kinds))
    single = len(outs) == 1
    return pl.pallas_call(
        kernel,
        out_shape=shapes[0] if single else shapes,
        in_specs=[near] * (ins - far_in) + [far] * far_in,
        out_specs=whole if single else (whole,) * (len(outs) - far_out) + (far,) * far_out,
        scratch_shapes=scratch,
        compiler_params=pltpu.CompilerParams(vmem_limit_bytes=int(mebibytes * 1024 * 1024)),
        cost_estimate=pl.CostEstimate(flops=flops, bytes_accessed=10**6, transcendentals=0),
    )


def packs():
    scratch = [vm((ROWS, COLS, SEG * CH), BF16)] * 2 + [vm((ROWS, COLS, N))] * 2
    scratch += [vm((ROWS, SEG, COLS))] * 2 + [pltpu.SemaphoreType.DMA((6,))]
    return call(pack_kernel, 6, [(SEG * SENT, 128)], scratch, 60, place=pltpu.HBM)


def edges(devices):
    outs = [(devices * EDGE, LANES), ENDS, TABLE, PLACE]
    scratch = [vm(WIDE), vm((TOKENS, LANES)), vm(RATES), vm(BLOCK), vm(FLIP, BF16)]
    return call(edges_kernel, 1, outs, scratch, 14, kinds=(F32, F32, F32, BF16))


def chains(devices):
    return call(chain_kernel, 1, [(devices, 2 * STEP, LANES)], [], 8)


def local_grads():
    outs = [(SEG * BACK, 128), (ROWS, LANES, LANES), (ROWS, LANES, LANES), WIDE, WIDE]
    scratch = [vm((COLS, 2 * LANES, 128), BF16), vm(WIDE), vm(WIDE), vm((COLS + 1,) + BLOCK), vm(ENDS)]
    scratch += [vm(BLOCK), vm(WIDE), vm((COLS, ROWS * CH, 2 * LANES), BF16), vm((4, ROWS, COLS, 8, LANES))]
    scratch += [vm(FLIP, BF16), vm((TOKENS, LANES)), vm(WIDE, BF16), pltpu.SemaphoreType.DMA((2,))]
    kinds = (F32, BF16, BF16, BF16, F32)
    return call(local_kernel, 4, outs, scratch, 50, kinds=kinds, flops=5 * 10**9, far_out=2)


def outer_grads():
    scratch = [vm(TOKEN), vm(TOKEN), vm(WIDE, BF16), vm(WIDE), vm(ENDS), vm((3, ROWS, COLS, 8, LANES)), vm(BLOCK)]
    scratch += [vm(BLOCK), vm((TOKENS, LANES)), vm((TOKENS, LANES)), vm((ROWS, LANES))]
    scratch += [pltpu.SemaphoreType.DMA((2, COLS))]
    return call(outer_kernel, 8, [(SEG * BACK, 128)], scratch, 50, far_in=2)


def unpacks():
    outs = [(ROWS, COLS, SEG * CH)] + [(ROWS, COLS, N)] * 2 + [(ROWS, SEG, COLS)] * 2
    return call(unpack_kernel, 1, outs, [], 8)


def exchange(a, axis):
    return lax.all_to_all(a.reshape(-1, 1, LANES), axis, 0, 0, tiled=True).reshape(-1, LANES)


def swapped(a):
    return jnp.transpose(a, (0, 2, 1))


def per_device(tokens, cotangent, state_in, state_out, width_decay, height_decay):
    devices = lax.axis_size("wa")
    message = packs()(
        tokens, cotangent, state_in, state_out, swapped(width_decay), swapped(height_decay)
    )
    tile = exchange(message, "ha")
    edge, back, table, place = edges(devices)(tile)
    edge = exchange(edge, "wa")
    local, high, low, *far = local_grads()(tile, back, place, table)
    carries = lax.all_to_all(chains(devices)(edge), "wa", 0, 0, tiled=True)
    answer = outer_grads()(tile, carries, local, table, high, low, *far)
    x, b, s, w, h = unpacks()(exchange(answer, "ha"))
    return x, b, s, swapped(w), swapped(h)


def solution(mesh):
    spec = P("ha", "wa", None)
    return jax.shard_map(
        per_device, mesh=mesh, in_specs=(spec,) * 6, out_specs=(spec,) * 5, check_vma=False
    )
```

```python
import jax
import jax.numpy as jnp
from jax import lax
from jax.experimental import pallas as pl
from jax.experimental.pallas import tpu as pltpu
from jax.sharding import PartitionSpec as P

F32 = jnp.float32
BF16 = jnp.bfloat16

SEG = 8
ROWS = 8
COLS = 16
CH = 64
N = 16
LANES = SEG * N
TOKENS = ROWS * COLS
STEP = 16
QUART = CH // STEP

X0, C0, B0, S0, D0 = 0, 64, 128, 144, 160
SENT = 162
I0, O0, W0 = 64, 80, 96
BACK = 98
EDGE = 33


def make_place(place):
    k = lax.broadcasted_iota(jnp.int32, (LANES, 256), 0)
    m = lax.broadcasted_iota(jnp.int32, (LANES, 256), 1)
    for two in range(COLS // 2):
        col = 2 * two + m // LANES
        hit = k == ((m % LANES) // N) * COLS + col
        place[two] = jnp.where(hit, 1.0, 0.0).astype(BF16)


def make_gather(gather):
    k = lax.broadcasted_iota(jnp.int32, (2 * LANES, 128), 0)
    m = lax.broadcasted_iota(jnp.int32, (2 * LANES, 128), 1)
    for col in range(COLS):
        hit = m == ((k % LANES) // N) * COLS + col
        gather[col] = jnp.where(hit, 1.0, 0.0).astype(BF16)


def take(ref, at, size, count):
    parts = [ref[g * count + at : g * count + at + size, :][None] for g in range(SEG)]
    return jnp.concatenate(parts, axis=0)


def give(ref, at, count, value):
    for g in range(SEG):
        ref[g * count + at : g * count + at + value.shape[1], :] = value[g]


def pack_kernel(x0, y0, b0, s0, w0, h0, out, x, y, b, s, w, h, done):
    copies = [
        pltpu.make_async_copy(source, target, done.at[k])
        for k, (source, target) in enumerate(((w0, w), (h0, h), (b0, b), (s0, s), (x0, x), (y0, y)))
    ]
    for copy in copies:
        copy.start()
    low = lax.broadcasted_iota(jnp.int32, (COLS, 128), 1) < CH
    for k, (at, a) in enumerate(((D0, w), (D0 + 1, h))):
        copies[k].wait()
        flat = jnp.concatenate([a[row] for row in range(ROWS)], axis=1)
        for g in range(SEG):
            out[g * SENT + at : g * SENT + at + 1, :] = flat[g : g + 1]
    for k, (at, a) in enumerate(((B0, b), (S0, s))):
        copies[2 + k].wait()
        flat = a[...].reshape(TOKENS, N).T
        for g in range(SEG):
            out[g * SENT + at : g * SENT + at + N, :] = flat
    for k, (at, a) in enumerate(((X0, x), (C0, y))):
        copies[4 + k].wait()
        for pair in range(ROWS // 2):
            to = at + pair * COLS
            for two in range(SEG // 2):
                lanes = slice(two * 128, (two + 1) * 128)
                one = a[2 * pair, :, lanes].astype(F32)
                other = a[2 * pair + 1, :, lanes].astype(F32)
                even, odd = 2 * two * SENT + to, (2 * two + 1) * SENT + to
                out[even : even + COLS, :] = jnp.where(low, one, pltpu.roll(other, CH, 1))
                out[odd : odd + COLS, :] = jnp.where(low, pltpu.roll(one, CH, 1), other)


def unpack_kernel(got, x, b, s, w, h):
    low = lax.broadcasted_iota(jnp.int32, (COLS, 128), 1) < CH
    for pair in range(ROWS // 2):
        for two in range(SEG // 2):
            lanes = slice(two * 128, (two + 1) * 128)
            even, odd = 2 * two * BACK + pair * COLS, (2 * two + 1) * BACK + pair * COLS
            one = got[even : even + COLS, :]
            other = got[odd : odd + COLS, :]
            x[2 * pair, :, lanes] = jnp.where(low, one, pltpu.roll(other, CH, 1))
            x[2 * pair + 1, :, lanes] = jnp.where(low, pltpu.roll(one, CH, 1), other)
    for at, a in ((I0, b), (O0, s)):
        flat = got[at : at + N, :]
        for g in range(1, SEG):
            flat = flat + got[g * BACK + at : g * BACK + at + N, :]
        a[...] = flat.T.reshape(ROWS, COLS, N)
    for at, a in ((W0, w), (W0 + 1, h)):
        flat = jnp.concatenate([got[g * BACK + at : g * BACK + at + 1, :] for g in range(SEG)], axis=0)
        for row in range(ROWS):
            a[row] = flat[:, row * COLS : (row + 1) * COLS]


def flip(ref, at, flipped):
    for pair in range(ROWS // 2):
        block = take(ref, at + pair * COLS, COLS, SENT).reshape(SEG * COLS, 2 * CH)
        flipped[pair * 2 * CH : (pair + 1) * 2 * CH, :] = block.T.astype(BF16)


def spread(flipped, place, wide, two, thin=None):
    for pair in range(ROWS // 2):
        block = flipped[pair * 2 * CH : (pair + 1) * 2 * CH, :]
        out = jnp.dot(block, place[two], preferred_element_type=F32)
        for part in range(2):
            for half in range(2):
                value = out[part * CH : (part + 1) * CH, half * LANES : (half + 1) * LANES]
                wide[2 * two + half, 2 * pair + part] = value
                if thin is not None:
                    thin[2 * two + half, 2 * pair + part] = value.astype(BF16)


def by_column(flat, out):
    for col in range(COLS):
        out[col] = flat[pl.ds(col, ROWS, stride=COLS), :]


def small(ref, flat, bt, ct, wr, hr):
    for at, out in ((B0, bt), (S0, ct)):
        flat[...] = take(ref, at, N, SENT).reshape(LANES, TOKENS).T
        by_column(flat, out)
    for at, out in ((D0, wr), (D0 + 1, hr)):
        rate = jnp.exp(take(ref, at, 1, SENT))
        flat[...] = jnp.broadcast_to(rate, (SEG, N, TOKENS)).reshape(LANES, TOKENS).T
        by_column(flat, out)


def tables(rows):
    return [rows.at[:, k * ROWS : (k + 1) * ROWS, :] for k in range(5)]


def mover(down):
    def move(v, by):
        return pltpu.roll(v, by * N if down else LANES - by * N, 1)

    return move


def inside(down):
    lane = lax.broadcasted_iota(jnp.int32, (1, LANES), 1)
    return (lane >= N) if down else (lane < LANES - N)


def carry_rates(flat, rates, down):
    move = mover(down)
    total = flat[0:COLS, :]
    for row in range(1, ROWS):
        total = total * flat[row * COLS : (row + 1) * COLS, :]
    one = jnp.where(inside(down), move(total, 1), 0.0)
    two = one * move(one, 1)
    rates[:, 0, :] = one
    rates[:, 1, :] = two
    rates[:, 2, :] = two * move(two, 2)


def carry_scan(ends, rates, down):
    move = mover(down)
    keep = inside(down)

    for part in range(1):
        cols = range(COLS)
        values = [jnp.where(keep, move(ends[col], 1), 0.0) for col in cols]
        for k, by in enumerate((1, 2, 4)):
            moved = [move(f, by) for f in values]
            values = [f + rates[col, k : k + 1, :] * g for col, f, g in zip(cols, values, moved)]
        for col, f in zip(cols, values):
            ends[col] = f


def split(v):
    high = v.astype(BF16)
    return high, (v - high.astype(F32)).astype(BF16)


def own_segment():
    r = lax.broadcasted_iota(jnp.int32, (LANES, LANES), 0)
    m = lax.broadcasted_iota(jnp.int32, (LANES, LANES), 1)
    return r // COLS == m // N


def diagonal(flat, row, own):
    value = flat[pl.ds(row, COLS, stride=ROWS), :]
    return jnp.where(own, jnp.concatenate([value] * SEG, axis=0), 0.0)


def edges_kernel(ref, edge, back, rows, place, ce, flat, rates, head, flipped):
    make_place(place)
    bt, ct, wr, hr, down = tables(rows)
    small(ref, flat, bt, ct, wr, hr)
    carry_rates(flat, rates, False)
    carry_rates(flat, down, True)
    flip(ref, C0, flipped)
    for two in range(COLS // 2):
        spread(flipped, place, ce, two)

    def ends(step, none):
        cols = [step * 4 + k for k in range(4)]
        carries = [jnp.zeros((CH, LANES), F32)] * 4
        for row in reversed(range(ROWS)):
            one = slice(row, row + 1)
            seeded = [ct[c, one, :] * ce[c, row] for c in cols]
            for c, v in zip(cols, seeded):
                ce[c, row] = v
            carries = [hr[c, one, :] * (v + seed) for c, v, seed in zip(cols, carries, seeded)]
        for c, v in zip(cols, carries):
            back[c] = v
        return none

    lax.fori_loop(0, COLS // 4, ends, 0)
    carry_scan(back, rates, False)

    after = jnp.ones((ROWS, LANES), F32)
    for col in reversed(range(COLS)):
        flat[col * ROWS : (col + 1) * ROWS, :] = after * bt[col]
        after = after * wr[col]
    own = own_segment()
    flip(ref, X0, flipped)
    for pair in range(ROWS // 2):
        for part in range(2):
            row = 2 * pair + part
            high, low = split(diagonal(flat, row, own))
            mine = flipped[row * CH : (row + 1) * CH, :]
            tail = jnp.dot(mine, high, preferred_element_type=F32) + jnp.dot(
                mine, low, preferred_element_type=F32
            )
            for q in range(QUART):
                at = (row * QUART + q) * EDGE
                edge[at : at + STEP, :] = tail[q * STEP : (q + 1) * STEP]
                edge[at + 2 * STEP : at + EDGE, :] = after[row : row + 1]

    head[...] = jnp.zeros_like(head)

    def sums(step, none):
        col = COLS - 1 - 2 * step
        carry, carry2 = back[col], back[col - 1]
        for row in reversed(range(ROWS)):
            one = slice(row, row + 1)
            grad = carry + ce[col, row]
            carry = hr[col, one, :] * grad
            grad2 = carry2 + ce[col - 1, row]
            carry2 = hr[col - 1, one, :] * grad2
            head[row] = wr[col - 1, one, :] * (wr[col, one, :] * (head[row] + grad) + grad2)
        return none

    lax.fori_loop(0, COLS // 2, sums, 0)
    for row in range(ROWS):
        for q in range(QUART):
            at = (row * QUART + q) * EDGE + STEP
            edge[at : at + STEP, :] = head[row, q * STEP : (q + 1) * STEP, :]


def chain_kernel(got, out):
    count = out.shape[0]
    right = left = jnp.zeros((STEP, LANES), F32)
    for hop in range(count):
        place = count - 1 - hop
        out[hop, 0:STEP, :] = right
        out[place, STEP : 2 * STEP, :] = left
        one, other = hop * EDGE, place * EDGE
        right = got[one + 2 * STEP : one + EDGE, :] * right + got[one : one + STEP, :]
        left = got[other + 2 * STEP : other + EDGE, :] * left + got[other + STEP : other + 2 * STEP, :]


def total8(v):
    v = v[0 : CH // 2] + v[CH // 2 :]
    v = v[0 : CH // 4] + v[CH // 4 :]
    return v[0:8] + v[8:16]


def local_kernel(
    ref, back, place, table, out, high, low, far_ce, far_grad,
    gather, xe, ce, states, front, run, kept, pieces, sums, flipped, flat, thin, done
):
    bt, ct, wr, hr, rates = tables(table)
    make_gather(gather)
    value = jnp.ones((ROWS, LANES), F32)
    for col in reversed(range(COLS)):
        flat[col * ROWS : (col + 1) * ROWS, :] = value * bt[col]
        value = value * wr[col]
    own = own_segment()
    for row in range(ROWS):
        high[row], low[row] = split(diagonal(flat, row, own))
    flip(ref, X0, flipped)
    for two in range(COLS // 2):
        spread(flipped, place, xe, two)
    flip(ref, C0, flipped)
    for two in range(COLS // 2):
        spread(flipped, place, ce, two, thin)
    copies = [
        pltpu.make_async_copy(source, target, done.at[k])
        for k, (source, target) in enumerate(((thin, far_ce), (kept, far_grad)))
    ]
    copies[0].start()
    states[0] = jnp.zeros(BLOCK, F32)
    run[...] = jnp.zeros(BLOCK, F32)

    def forward(col, none):
        total = jnp.zeros((CH, LANES), F32)
        for row in range(ROWS):
            one = slice(row, row + 1)
            state = wr[col, one, :] * states[col, row] + bt[col, one, :] * xe[col, row]
            states[col + 1, row] = state
            total = hr[col, one, :] * total + state
        front[col] = total
        return none

    lax.fori_loop(0, COLS, forward, 0)
    carry_scan(front, rates, True)

    def products(step, none):
        col = COLS - 1 - step
        carry = back[col]
        for row in reversed(range(ROWS)):
            one = slice(row, row + 1)
            grad = carry + ct[col, one, :] * ce[col, row]
            carry = hr[col, one, :] * grad
            kept[col, row] = grad
        total = front[col]
        for row in range(ROWS):
            one = slice(row, row + 1)
            grad = kept[col, row]
            sums[3, row, col] = total8(grad * total)
            total = hr[col, one, :] * total + states[col + 1, row]
            sums[1, row, col] = total8(total * ce[col, row])
            grad = grad + run[row]
            run[row] = wr[col, one, :] * grad
            sums[2, row, col] = total8(grad * states[col, row])
            sums[0, row, col] = total8(grad * xe[col, row])
            high, low = split(grad * bt[col, one, :])
            pieces[col, row * CH : (row + 1) * CH, 0:LANES] = high
            pieces[col, row * CH : (row + 1) * CH, LANES:] = low
        return none

    lax.fori_loop(0, COLS, products, 0)
    copies[1].start()
    for pair in range(ROWS // 2):
        rows = slice(pair * 2 * CH, (pair + 1) * 2 * CH)
        block = jnp.zeros((2 * CH, 128), F32)
        for col in range(COLS):
            block = block + jnp.dot(pieces[col, rows, :], gather[col], preferred_element_type=F32)
        give(out, pair * COLS, BACK, block.T.reshape(SEG, COLS, 2 * CH))
    for which, at in enumerate((I0, O0, W0, W0 + 1)):
        put(ref, out, at, over_sublanes(sums.at[which]))
    for copy in copies:
        copy.wait()


def over_sublanes(part):
    rows = part.reshape(TOKENS * 8, LANES)
    value = rows[pl.ds(0, TOKENS, stride=8), :]
    for k in range(1, 8):
        value = value + rows[pl.ds(k, TOKENS, stride=8), :]
    return value


def put(ref, out, at, value, old=None):
    value = value.T.reshape(SEG, N, TOKENS)
    size = N
    if at >= W0:
        rate = jnp.exp(take(ref, D0 + at - W0, 1, SENT))
        value, size = rate * jnp.sum(value, axis=1, keepdims=True), 1
    if old is not None:
        value = value + take(old, at, size, BACK)
    give(out, at, BACK, value)


def outer_kernel(
    ref, edge, local, table, high, low, far_ce, far_grad, out,
    before, after, ce, inner, front, sums, left, right, flat, raw, meet, entered, done
):
    def fetch(col):
        return (
            pltpu.make_async_copy(far_grad.at[col], inner.at[col], done.at[0, col]),
            pltpu.make_async_copy(far_ce.at[col], ce.at[col], done.at[1, col]),
        )

    for col in range(COLS):
        for copy in fetch(col):
            copy.start()
    bt, ct, wr, hr, rates = tables(table)
    value = jnp.ones((ROWS, LANES), F32)
    for col in range(COLS):
        value = value * wr[col]
        before[col] = value
    value = jnp.ones((ROWS, LANES), F32)
    for col in reversed(range(COLS)):
        after[col] = value
        value = value * wr[col]
    for row in range(ROWS):
        for q in range(QUART):
            part = slice(q * STEP, (q + 1) * STEP)
            left[row, part, :] = edge[row * QUART + q, 0:STEP, :]
            right[row, part, :] = edge[row * QUART + q, STEP : 2 * STEP, :]

    own = own_segment()
    empty = jnp.zeros((CH, LANES), BF16)
    half = lax.broadcasted_iota(jnp.int32, (LANES, 128), 1) < CH
    for pair in range(ROWS // 2):
        tokens = take(ref, X0 + pair * COLS, COLS, SENT).reshape(SEG * COLS, 2 * CH).astype(BF16)
        parts = [split(right[2 * pair + part]) for part in range(2)]
        both = [jnp.concatenate([parts[0][k], parts[1][k]], axis=0) for k in range(2)]
        found = []
        for part in range(2):
            row = 2 * pair + part
            value = jnp.zeros((LANES, LANES), F32)
            for k in range(2):
                pieces = [parts[0][k], empty] if part == 0 else [empty, parts[1][k]]
                value = value + jnp.dot(tokens, jnp.concatenate(pieces, axis=0), preferred_element_type=F32)
            value = jnp.where(own, value, 0.0).reshape(SEG, COLS, LANES)
            raw[row * COLS : (row + 1) * COLS, :] = jnp.sum(value, axis=0)
            meet[row : row + 1, :] = jnp.sum(right[row] * left[row], axis=0, keepdims=True)
            value = jnp.zeros((LANES, 128), F32)
            for weight, k in ((low, 0), (high, 1), (high, 0)):
                value = value + lax.dot_general(
                    weight[row], both[k], (((1,), (1,)), ((), ())), preferred_element_type=F32
                )
            found.append(value)
        value = jnp.where(half, found[0], found[1]).reshape(SEG, COLS, 128)
        give(out, pair * COLS, BACK, take(local, pair * COLS, COLS, BACK) + value)

    def forward(step, none):
        cols = [step * 4 + k for k in range(4)]
        totals = [jnp.zeros((CH, LANES), F32)] * 4
        for row in range(ROWS):
            one = slice(row, row + 1)
            enter = left[row]
            parts = [before[c, one, :] * enter for c in cols]
            for c, v in zip(cols, parts):
                entered[c, row] = v
            totals = [hr[c, one, :] * v + part for c, v, part in zip(cols, totals, parts)]
        for c, v in zip(cols, totals):
            front[c] = v
        return none

    lax.fori_loop(0, COLS // 4, forward, 0)
    carry_scan(front, rates, True)

    def products(col, none):
        for copy in fetch(col):
            copy.wait()
        total = front[col]
        for row in range(ROWS):
            one = slice(row, row + 1)
            grad = inner[col, row]
            sums[2, row, col] = total8(grad * left[row])
            sums[1, row, col] = total8(grad * total)
            total = hr[col, one, :] * total + entered[col, row]
            sums[0, row, col] = total8(total * ce[col, row].astype(F32))
        return none

    lax.fori_loop(0, COLS, products, 0)

    put(ref, out, O0, over_sublanes(sums.at[0]), local)
    put(ref, out, W0 + 1, over_sublanes(sums.at[1]), local)
    flat[...] = over_sublanes(sums.at[2])

    def rows_of(a, col):
        return a[pl.ds(col, ROWS, stride=COLS), :]

    value = jnp.zeros((ROWS, LANES), F32)
    terms = [None] * COLS
    for col in reversed(range(COLS)):
        value = rows_of(flat, col) + value
        terms[col] = value * before[col - 1] if col else value
        value = wr[col] * value
    value = meet[...]
    for col in range(COLS):
        terms[col] = terms[col] + after[col] * value
        product = rows_of(raw, col)
        value = wr[col] * value + bt[col] * product
        raw[pl.ds(col, ROWS, stride=COLS), :] = after[col] * product
    for col in range(COLS):
        flat[pl.ds(col, ROWS, stride=COLS), :] = terms[col]
    put(ref, out, I0, raw[...], local)
    put(ref, out, W0, flat[...], local)


WIDE = (COLS, ROWS, CH, LANES)
TOKEN = (COLS, ROWS, LANES)
ENDS = (COLS, CH, LANES)
BLOCK = (ROWS, CH, LANES)
RATES = (COLS, ROWS, LANES)
TABLE = (COLS, 5 * ROWS, LANES)
PLACE = (COLS // 2, LANES, 256)
FLIP = (ROWS * CH, 128)


def vm(shape, kind=F32):
    return pltpu.VMEM(shape, kind)


def call(kernel, ins, outs, scratch, mebibytes, kinds=None, place=pltpu.VMEM, flops=10**8, far_in=0, far_out=0):
    near, far = pl.BlockSpec(memory_space=place), pl.BlockSpec(memory_space=pltpu.HBM)
    whole = pl.BlockSpec(memory_space=pltpu.VMEM)
    kinds = kinds or (F32,) * len(outs)
    shapes = tuple(jax.ShapeDtypeStruct(s, k) for s, k in zip(outs, kinds))
    single = len(outs) == 1
    return pl.pallas_call(
        kernel,
        out_shape=shapes[0] if single else shapes,
        in_specs=[near] * (ins - far_in) + [far] * far_in,
        out_specs=whole if single else (whole,) * (len(outs) - far_out) + (far,) * far_out,
        scratch_shapes=scratch,
        compiler_params=pltpu.CompilerParams(vmem_limit_bytes=int(mebibytes * 1024 * 1024)),
        cost_estimate=pl.CostEstimate(flops=flops, bytes_accessed=10**6, transcendentals=0),
    )


def packs():
    scratch = [vm((ROWS, COLS, SEG * CH), BF16)] * 2 + [vm((ROWS, COLS, N))] * 2
    scratch += [vm((ROWS, SEG, COLS))] * 2 + [pltpu.SemaphoreType.DMA((6,))]
    return call(pack_kernel, 6, [(SEG * SENT, 128)], scratch, 60, place=pltpu.HBM)


def edges(devices):
    outs = [(devices * EDGE, LANES), ENDS, TABLE, PLACE]
    scratch = [vm(WIDE), vm((TOKENS, LANES)), vm(RATES), vm(BLOCK), vm(FLIP, BF16)]
    return call(edges_kernel, 1, outs, scratch, 14, kinds=(F32, F32, F32, BF16))


def chains(devices):
    return call(chain_kernel, 1, [(devices, 2 * STEP, LANES)], [], 8)


def local_grads():
    outs = [(SEG * BACK, 128), (ROWS, LANES, LANES), (ROWS, LANES, LANES), WIDE, WIDE]
    scratch = [vm((COLS, 2 * LANES, 128), BF16), vm(WIDE), vm(WIDE), vm((COLS + 1,) + BLOCK), vm(ENDS)]
    scratch += [vm(BLOCK), vm(WIDE), vm((COLS, ROWS * CH, 2 * LANES), BF16), vm((4, ROWS, COLS, 8, LANES))]
    scratch += [vm(FLIP, BF16), vm((TOKENS, LANES)), vm(WIDE, BF16), pltpu.SemaphoreType.DMA((2,))]
    kinds = (F32, BF16, BF16, BF16, F32)
    return call(local_kernel, 4, outs, scratch, 50, kinds=kinds, flops=5 * 10**9, far_out=2)


def outer_grads():
    scratch = [vm(TOKEN), vm(TOKEN), vm(WIDE, BF16), vm(WIDE), vm(ENDS), vm((3, ROWS, COLS, 8, LANES)), vm(BLOCK)]
    scratch += [vm(BLOCK), vm((TOKENS, LANES)), vm((TOKENS, LANES)), vm((ROWS, LANES))]
    scratch += [vm(WIDE), pltpu.SemaphoreType.DMA((2, COLS))]
    return call(outer_kernel, 8, [(SEG * BACK, 128)], scratch, 50, far_in=2)


def unpacks():
    outs = [(ROWS, COLS, SEG * CH)] + [(ROWS, COLS, N)] * 2 + [(ROWS, SEG, COLS)] * 2
    return call(unpack_kernel, 1, outs, [], 8)


def exchange(a, axis):
    return lax.all_to_all(a.reshape(-1, 1, LANES), axis, 0, 0, tiled=True).reshape(-1, LANES)


def swapped(a):
    return jnp.transpose(a, (0, 2, 1))


def per_device(tokens, cotangent, state_in, state_out, width_decay, height_decay):
    devices = lax.axis_size("wa")
    message = packs()(
        tokens, cotangent, state_in, state_out, swapped(width_decay), swapped(height_decay)
    )
    tile = exchange(message, "ha")
    edge, back, table, place = edges(devices)(tile)
    edge = exchange(edge, "wa")
    local, high, low, *far = local_grads()(tile, back, place, table)
    carries = lax.all_to_all(chains(devices)(edge), "wa", 0, 0, tiled=True)
    answer = outer_grads()(tile, carries, local, table, high, low, *far)
    x, b, s, w, h = unpacks()(exchange(answer, "ha"))
    return x, b, s, swapped(w), swapped(h)


def solution(mesh):
    spec = P("ha", "wa", None)
    return jax.shard_map(
        per_device, mesh=mesh, in_specs=(spec,) * 6, out_specs=(spec,) * 5, check_vma=False
    )
```
